32 devices in a mesh: dp: 4 (over z), expert: 8 (over y, x, core).
Axes of the slice: x: 2, y: 2, z: 4, core: 2. Of those that a mesh axis runs over, the one named last changes fastest.
Arguments:
- hidden: bfloat16 [32768, 768], P(('dp', 'expert')), may hold values from -6 to 6
- grad_out: bfloat16 [32768, 2048], P(('dp', 'expert')), may hold values from -0.19921875 to 0.19921875
- block_slot: int32 [32, 8], P(('dp', 'expert')), may hold values from 0 to 2, as said below
- block_count: int32 [32], P(('dp', 'expert')), may hold values from 2 to 8, as said below
- replica_expert: int32 [8], replicated, may hold values from 0 to 15, as said below
Outputs:
- grad_down: bfloat16 [16, 768, 2048], P('expert', None, 'dp')
The draws below stay inside these ranges and needn't reach their ends.
Inputs may be any that keep to these rules, and one draw needn't show every extreme that they name: `replica_expert`: Expert-axis index k is home to experts k * 2 to k * 2 + 1 and has one replica slot. The indices holding an expert homed at h are h alone, or h and (h + 4) mod 8, or h and (h + m * 2) mod 8 for m = 1, 2, 3; in every draw some expert homed at index 7 has such a set of four. `block_count`: some device has all 8 blocks live. `block_slot`: block 0 of every device belongs to the replica slot 2.
All inputs are finite; a program needn't handle non-finite values.
Results may differ from the reference program's by a relative error of at most 0.0065.
Values may be sent and summed in bfloat16 or wider, within the bound.
No kernel may reach another device: no remote copies, remote signals or barrier semaphores. Data moves between devices by JAX's collectives and lax.ppermute only.
A program may use at most 128 MiB of HBM per device.

```python
import jax
import jax.numpy as jnp
from jax import lax

FF = 768
DW = 2048
EXP_DEV = 2
BLOCK = 128
BLOCKS = 8
HOSTS = 8
SHARDS = 4
EXPERTS = 16
TOKENS = 32768


def placement_table(key):
    quarter = HOSTS // 4
    base = jax.random.fold_in(key, 11)
    kind_key, home_key, local_key, four_key = jax.random.split(base, 4)
    groups = jnp.arange(quarter)
    kinds = jax.random.randint(kind_key, (quarter,), 0, 2)
    kinds = jnp.where((groups == 0) | (groups == quarter - 1), 1, kinds)
    home_pos = jax.random.randint(home_key, (quarter,), 0, 4)
    home_pos = jnp.where(groups == quarter - 1, 3, home_pos)
    local_pick = jax.random.randint(local_key, (quarter, 4), 0, EXP_DEV)
    four_pick = jax.random.randint(four_key, (quarter,), 0, EXP_DEV)
    column = jnp.arange(4)[None, :]
    group = groups[:, None]
    partner = (column + 2) % 4
    paired = (group + partner * quarter) * EXP_DEV + local_pick
    fourfold = (groups + home_pos * quarter) * EXP_DEV + four_pick
    use_four = (kinds[:, None] == 1) & (column != home_pos[:, None])
    chosen = jnp.where(use_four, fourfold[:, None], paired)
    return chosen.T.reshape(-1).astype(jnp.int32)


def draw_replica_expert(key, part):
    return placement_table(key)


def draw_block_slot(key, part):
    slot_key = jax.random.fold_in(key, 5)
    devices = SHARDS * HOSTS
    slots = jax.random.randint(slot_key, (devices, BLOCKS), 0, EXP_DEV + 1)
    first = jnp.arange(BLOCKS)[None, :] == 0
    return jnp.where(first, EXP_DEV, slots).astype(jnp.int32)


def draw_block_count(key, part):
    count_key = jax.random.fold_in(key, 7)
    devices = SHARDS * HOSTS
    counts = jax.random.randint(count_key, (devices,), max(1, BLOCKS // 4), BLOCKS + 1)
    counts = jnp.where(jnp.arange(devices) == 0, BLOCKS, counts)
    return counts.astype(jnp.int32)


def steps_of(own_key, shape, cuts, smallest, largest):
    gain, own = 1.0, jax.random.fold_in(own_key, 6)
    for dim, shards_of in cuts:
        steps = jnp.exp(jax.random.uniform(jax.random.fold_in(own, dim), (shards_of,), jnp.float32, smallest / len(cuts), largest / len(cuts)))
        gain = gain * jnp.repeat(steps, shape[dim] // shards_of).reshape([-1 if axis == dim else 1 for axis in range(len(shape))])
    return gain


def normal_values(rng, dims, spread, most, cuts=(), kind=jnp.bfloat16):
    entries = spread * jax.random.normal(rng, dims, jnp.float32)
    if cuts:
        entries = entries * steps_of(rng, dims, cuts, -0.22, 0.18)
    return jnp.clip(entries, -most, most).astype(kind)


def setup_inputs(seed: int = 0) -> dict:
    arg_keys = jax.random.split(jax.random.key(seed), 6)
    return {
        "hidden": normal_values(arg_keys[0], (TOKENS, FF), 1.0, 6.0, ((0, 32),)),
        "grad_out": normal_values(arg_keys[1], (TOKENS, DW), 0.03, 0.19921875, ((0, 32),)),
        "block_slot": draw_block_slot(jax.random.fold_in(arg_keys[5], 71), 0),
        "block_count": draw_block_count(jax.random.fold_in(arg_keys[5], 71), 0),
        "replica_expert": draw_replica_expert(jax.random.fold_in(arg_keys[5], 71), 0),
    }


def reference(hidden, grad_out, block_slot, block_count, replica_expert):
    total_blocks = hidden.shape[0] // BLOCK
    rows_in = hidden.reshape(total_blocks, BLOCK, FF)
    rows_out = grad_out.reshape(total_blocks, BLOCK, DW)
    position = jnp.arange(total_blocks, dtype=jnp.int32)
    device = position // BLOCKS
    holder = device % HOSTS
    slot_ids = block_slot.reshape(-1).astype(jnp.int32)
    owners = jnp.where(slot_ids < EXP_DEV, holder * EXP_DEV + slot_ids, replica_expert[holder]).astype(jnp.int32)
    block_live = (position % BLOCKS) < block_count[device]

    def add_block(totals, block_item):
        block_in, block_out, owner, live_flag = block_item

        def accumulate(current):
            product = jnp.dot(block_in.T, block_out, preferred_element_type=jnp.float32)
            return current.at[owner].add(product)

        def unchanged(current):
            return current

        return lax.cond(live_flag, accumulate, unchanged, totals), None

    totals = jnp.zeros((EXPERTS, FF, DW), jnp.float32)
    totals, _ = lax.scan(add_block, totals, (rows_in, rows_out, owners, block_live))
    return totals.astype(jnp.bfloat16)
```

```python
import functools

import jax
import jax.numpy as jnp
from jax import lax
from jax.experimental import pallas as pl
from jax.experimental.pallas import tpu as pltpu
from jax.sharding import PartitionSpec as P

EXP_DEV = 2
COLD, HOT, REPLICA = 0, 1, 2


class Route:
    def __init__(self, placement, dp, expert, holders):
        quarter = holders // 4
        group, place = lax.rem(expert, quarter), lax.div(expert, quarter)

        def at(flip):
            return jnp.bitwise_xor(place, flip) * quarter + group

        self.d = dp
        self.here = expert
        self.near = {flip: at(flip) for flip in (1, 2, 3)}
        self.mine = placement[expert]
        self.theirs = {flip: placement[self.near[flip]] for flip in (1, 2, 3)}
        hot = jnp.int32(EXP_DEV - 1)
        for flip in (3, 1, 2):
            owner = self.theirs[flip]
            hot = jnp.where(self.home(owner) == expert, lax.rem(owner, EXP_DEV), hot)
        self.hot = hot
        self.at_home = self.home(self.mine) == expert

    def home(self, owner):
        return lax.div(owner, EXP_DEV)

    def kind(self, slot):
        local = jnp.where((slot == EXP_DEV) & self.at_home, lax.rem(self.mine, EXP_DEV), slot)
        return jnp.where(local == EXP_DEV, REPLICA, jnp.where(local == self.hot, HOT, COLD))

    def arrives(self, flip):
        return self.home(self.theirs[flip]) == self.here

    def passes(self, first, second):
        return self.home(self.theirs[first]) == self.near[second]

    def goes(self, flip):
        return self.home(self.mine) == self.near[flip]


def piece_kernel(jobs, holders, width, n_in, *refs):
    slots, counts, placement, hidden, grad = refs[:5]
    arrived = refs[5 : 5 + n_in]
    n_out = sum(len(job["rows"]) for job in jobs)
    outs = refs[5 + n_in : 5 + n_in + n_out]
    hidden_v, grad_v, total, sem = refs[5 + n_in + n_out :]
    blocks = slots.shape[1]
    rows = hidden.shape[0] // blocks
    route = Route(placement, lax.axis_index("dp"), lax.axis_index("expert"), holders)
    fetch = pltpu.make_async_copy(hidden, hidden_v, sem.at[0])
    fetch.start()
    columns = []
    for j, job in enumerate(jobs):
        begin = pl.multiple_of(job["column"](route.d) * width, width)
        columns.append(pltpu.make_async_copy(grad.at[:, pl.ds(begin, width)], grad_v.at[j], sem.at[1 + j]))
        columns[-1].start()
    fetch.wait()
    outs = list(outs)
    for j, job in enumerate(jobs):
        columns[j].wait()
        total[...] = jnp.zeros_like(total)

        @pl.loop(0, blocks)
        def _(b):
            @pl.when((b < counts[0]) & (route.kind(slots[0, b]) == job["kind"]))
            def _():
                at = pl.ds(pl.multiple_of(b * rows, rows), rows)
                total[...] += lax.dot_general(
                    hidden_v[at, :], grad_v[j, at, :], (((0,), (0,)), ((), ())), preferred_element_type=jnp.float32
                )

        for position, part, index, when in job["adds"]:
            chosen = arrived[position] if index is None else arrived[position].at[index]

            def add(chosen=chosen, part=part):
                total[part, :] += chosen[...].astype(jnp.float32)

            if when is None:
                add()
            else:
                pl.when(when(route))(add)
        for part in job["rows"]:
            outs.pop(0)[...] = total[part, :].astype(jnp.bfloat16)


def make_pieces(jobs, env, arrived=()):
    hidden, grad, slots, counts, placement, holders, width = env
    ff = hidden.shape[1]
    shapes = [(part.stop - part.start, width) for job in jobs for part in job["rows"]]
    smem, vmem, anywhere = (pl.BlockSpec(memory_space=space) for space in (pltpu.SMEM, pltpu.VMEM, pl.ANY))
    return pl.pallas_call(
        functools.partial(piece_kernel, jobs, holders, width, len(arrived)),
        out_shape=[jax.ShapeDtypeStruct(shape, jnp.bfloat16) for shape in shapes],
        in_specs=[smem, smem, smem, anywhere, anywhere] + [vmem] * len(arrived),
        out_specs=[vmem] * len(shapes),
        scratch_shapes=[
            pltpu.VMEM(hidden.shape, hidden.dtype),
            pltpu.VMEM((len(jobs), hidden.shape[0], width), grad.dtype),
            pltpu.VMEM((ff, width), jnp.float32),
            pltpu.SemaphoreType.DMA((1 + len(jobs),)),
        ],
        compiler_params=pltpu.CompilerParams(vmem_limit_bytes=32 << 20),
        cost_estimate=pl.CostEstimate(
            flops=len(jobs) * hidden.shape[0] * ff * width,
            bytes_accessed=2 * (hidden.size + len(jobs) * (hidden.shape[0] + ff) * width),
            transcendentals=0,
        ),
    )(slots, counts, placement, hidden, grad, *arrived)


def relay_kernel(holders, legs, placement, *refs):
    route = Route(placement, lax.axis_index("dp"), lax.axis_index("expert"), holders)
    for i, (first, second) in enumerate(legs):
        own, came, out = refs[i], refs[len(legs) + i], refs[2 * len(legs) + i]
        mine, other = route.goes(second), route.passes(first, second)
        zero = jnp.zeros(own.shape, jnp.float32)
        out[...] = (
            jnp.where(mine, own[...].astype(jnp.float32), zero) + jnp.where(other, came[...].astype(jnp.float32), zero)
        ).astype(out.dtype)


def relay(placement, holders, legs, own, came):
    smem, vmem = pl.BlockSpec(memory_space=pltpu.SMEM), pl.BlockSpec(memory_space=pltpu.VMEM)
    return pl.pallas_call(
        functools.partial(relay_kernel, holders, legs),
        out_shape=[jax.ShapeDtypeStruct(a.shape, a.dtype) for a in own],
        in_specs=[smem] + [vmem] * (2 * len(legs)),
        out_specs=[vmem] * len(legs),
        compiler_params=pltpu.CompilerParams(vmem_limit_bytes=32 << 20),
        cost_estimate=pl.CostEstimate(flops=sum(a.size for a in own), bytes_accessed=6 * sum(a.size for a in own), transcendentals=0),
    )(placement, *own, *came)


def flip_pairs(holders, flip):
    quarter = holders // 4
    return [(k, ((k // quarter) ^ flip) * quarter + k % quarter) for k in range(holders)]


def finish_kernel(hot_ref, cold, hot, out):
    at = hot_ref[0]
    out[1 - at] = cold[...]
    out[at] = hot[...]


def body(hidden, grad, slots, counts, placement):
    n, holders = lax.axis_size("dp"), lax.axis_size("expert")
    ff, width = hidden.shape[1], grad.shape[1] // n
    env = (hidden, grad, slots, counts, placement, holders, width)
    half = ff // 2
    whole, halves = slice(0, ff), (slice(0, half), slice(half, ff))
    legs = ((1, 2), (2, 1))

    def right_column(t):
        return lambda d: jnp.clip(n - t + d, 0, n - 1)

    def left_column(t):
        return lambda d: jnp.clip(t - n + d, 0, n - 1)

    def round_job(mask):
        return {"kind": REPLICA, "column": lambda d: jnp.bitwise_xor(d, mask), "rows": halves, "adds": []}

    def first_job(kind, adds=()):
        return {"kind": kind, "column": lambda d: jnp.where(d == 0, n - 1, 0), "rows": (whole,), "adds": list(adds)}

    def hop(x, flip):
        return lax.ppermute(x, "expert", flip_pairs(holders, flip))

    def swap(own):
        came = [hop(a, first) for a, (first, _) in zip(own, legs)]
        relayed = relay(placement, holders, legs, own, came)
        second = [hop(a, second) for a, (_, second) in zip(relayed, legs)]
        return list(came) + list(second)

    def plane_adds(base, columns, masks):
        adds = []
        for i, mask in enumerate(masks):
            for leg, (first, second) in enumerate(legs):
                here = lambda r, mask=mask: jnp.bitwise_xor(r.d, mask) == columns(r.d)
                adds.append((base + 4 * i + leg, halves[leg], None, lambda r, h=here, f=first: h(r) & r.arrives(f)))
                adds.append((base + 4 * i + 2 + leg, halves[leg], None, here))
        return adds

    def step_masks(t):
        right = sorted({(n - t + d) ^ d for d in range(t)})
        left = sorted({(t - n + d) ^ d for d in range(n - t, n)})
        return right, left

    def send(x, pairs):
        return lax.ppermute(x, "dp", pairs)

    def right_pairs(t):
        return [(d, d + 1) for d in range(t)]

    def left_pairs(t):
        return [(n - 1 - d, n - 2 - d) for d in range(t)]

    def step(kind, t, came_right, came_left, planes):
        right, left = step_masks(t)
        arrived = [came_right] + ([came_left] if came_left is not came_right else [])
        r_adds, l_adds = [(0, whole, None, None)], [(len(arrived) - 1, whole, None, None)]
        if planes is not None:
            masks = sorted(set(right) | set(left))
            base = len(arrived)
            arrived = arrived + [a for mask in masks for a in planes[mask]]
            r_adds += [x for x in plane_adds(base, right_column(t), masks)]
            l_adds += [x for x in plane_adds(base, left_column(t), masks)]
        jobs = [
            {"kind": kind, "column": right_column(t), "rows": (whole,), "adds": r_adds},
            {"kind": kind, "column": left_column(t), "rows": (whole,), "adds": l_adds},
        ]
        r, l = make_pieces(jobs, env, arrived)
        return send(r, right_pairs(t)), send(l, left_pairs(t))

    def last(kind, came_right, came_left, planes):
        adds, arrived = [(0, whole, None, None), (1, whole, None, None)], [came_right, came_left]
        if planes is not None:
            adds += plane_adds(2, lambda d: d, [0])
            arrived = arrived + list(planes[0])
        job = {"kind": kind, "column": lambda d: d, "rows": (whole,), "adds": adds}
        return make_pieces([job], env, arrived)[0]

    planes = {}
    first_pairs = [(0, 1), (n - 1, n - 2)]
    cold_1, *own = make_pieces([first_job(COLD), round_job(n - 1)], env)
    cold_r = cold_l = send(cold_1, first_pairs)
    planes[n - 1] = swap(own)
    for mask in range(n - 2, -1, -1):
        planes[mask] = swap(make_pieces([round_job(mask)], env))
    hot_adds = plane_adds(0, lambda d: jnp.where(d == 0, n - 1, 0), [n - 1])
    (hot_1,) = make_pieces([first_job(HOT, hot_adds)], env, planes[n - 1])
    hot_r = hot_l = send(hot_1, first_pairs)
    for t in range(2, n):
        cold_r, cold_l = step(COLD, t, cold_r, cold_l, None)
        hot_r, hot_l = step(HOT, t, hot_r, hot_l, planes)
    cold = last(COLD, cold_r, cold_l, None)
    hot = last(HOT, hot_r, hot_l, planes)
    route = Route(placement, lax.axis_index("dp"), lax.axis_index("expert"), holders)
    first = jnp.where(route.hot == 0, hot, cold)
    second = jnp.where(route.hot == 0, cold, hot)
    return jnp.stack([first, second])


def solution(mesh):
    in_specs = (
        P(("dp", "expert"), None),
        P(("dp", "expert"), None),
        P(("dp", "expert"), None),
        P(("dp", "expert")),
        P(),
    )
    out_specs = P("expert", None, "dp")
    return jax.shard_map(body, mesh=mesh, in_specs=in_specs, out_specs=out_specs, check_vma=False)
```

```python
import functools

import jax
import jax.numpy as jnp
from jax import lax
from jax.experimental import pallas as pl
from jax.experimental.pallas import tpu as pltpu
from jax.sharding import PartitionSpec as P

EXP_DEV = 2
COLD, HOT, REPLICA = 0, 1, 2
SMEM = pl.BlockSpec(memory_space=pltpu.SMEM)
VMEM = pl.BlockSpec(memory_space=pltpu.VMEM)
ANY = pl.BlockSpec(memory_space=pl.ANY)
HBM = pl.BlockSpec(memory_space=pltpu.HBM)


def params(mib):
    return pltpu.CompilerParams(vmem_limit_bytes=mib << 20)


def flip_of(k, quarter, phase):
    return 1 + (k % quarter + phase) % 2


def partner(k, quarter, flip):
    return jnp.bitwise_xor(k // quarter, flip) * quarter + k % quarter


F_HOT, F_GOES, F_PASSES, F_ARRIVES, F_COUNT = 0, 1, 2, 3, 4


def write_flags(flags, slots, counts, placement, blocks, holders):
    here = lax.axis_index("expert")
    quarter = holders // 4
    group, place = lax.rem(here, quarter), lax.div(here, quarter)

    def at(flip):
        return jnp.bitwise_xor(place, flip) * quarter + group

    def home(owner):
        return lax.div(owner, EXP_DEV)

    odd = lax.rem(group, 2)
    first, second = 1 + odd, 2 - odd
    mine, sender = placement[here], placement[at(first)]
    hot = jnp.int32(EXP_DEV - 1)
    for flip in (3, 1, 2):
        owner = placement[at(flip)]
        hot = jnp.where(home(owner) == here, lax.rem(owner, EXP_DEV), hot)
    flags[blocks + F_HOT] = hot
    flags[blocks + F_GOES] = (home(mine) == at(second)).astype(jnp.int32)
    flags[blocks + F_PASSES] = (home(sender) == at(second)).astype(jnp.int32)
    flags[blocks + F_ARRIVES] = (home(sender) == here).astype(jnp.int32)
    for b in range(blocks):
        slot = slots[0, b]
        local = jnp.where((slot == EXP_DEV) & (home(mine) == here), lax.rem(mine, EXP_DEV), slot)
        kind = jnp.where(local == EXP_DEV, REPLICA, jnp.where(local == hot, HOT, COLD))
        flags[b] = jnp.where(b < counts[0], kind, -1)


def products(jobs, blocks, flags, hidden_v, grad_v, total, outs, wait):
    rows = hidden_v.shape[0] // blocks
    for j, (kind, _) in enumerate(jobs):
        wait(j)
        total[...] = jnp.zeros_like(total)

        @pl.loop(0, blocks)
        def _(b):
            @pl.when(flags[b] == kind)
            def _():
                at = pl.ds(pl.multiple_of(b * rows, rows), rows)
                total[...] += lax.dot_general(
                    hidden_v[at, :], grad_v[j, at, :], (((0,), (0,)), ((), ())), preferred_element_type=jnp.float32
                )

        outs[j][...] = total[...].astype(outs[j].dtype)


def fetches(jobs, hidden, grad, hidden_v, grad_v, sem):
    width = grad_v.shape[2]
    copies = [pltpu.make_async_copy(hidden, hidden_v, sem.at[0])]
    for j, (_, mask) in enumerate(jobs):
        begin = pl.multiple_of(jnp.bitwise_xor(lax.axis_index("dp"), mask) * width, width)
        copies.append(pltpu.make_async_copy(grad.at[:, pl.ds(begin, width)], grad_v.at[j], sem.at[1 + j]))
    for copy in copies:
        copy.start()

    def wait(j):
        if j == 0:
            copies[0].wait()
        copies[1 + j].wait()

    return wait


def opening_kernel(jobs, blocks, holders, slots, counts, placement, hidden, grad, flags, *refs):
    outs = refs[: len(jobs)]
    slots_s, counts_s, placement_s, hidden_v, grad_v, total, sem, small = refs[len(jobs) :]
    scalars = [
        pltpu.make_async_copy(source, target, small.at[i])
        for i, (source, target) in enumerate(((slots, slots_s), (counts, counts_s), (placement, placement_s)))
    ]
    for copy in scalars:
        copy.start()
    wait = fetches(jobs, hidden, grad, hidden_v, grad_v, sem)
    for copy in scalars:
        copy.wait()
    write_flags(flags, slots_s, counts_s, placement_s, blocks, holders)
    products(jobs, blocks, flags, hidden_v, grad_v, total, outs, wait)


def product_kernel(jobs, blocks, flags, hidden, grad, *refs):
    outs = refs[1 : 1 + len(jobs)]
    hidden_v, grad_v, total, sem = refs[1 + len(jobs) :]
    wait = fetches(jobs, hidden, grad, hidden_v, grad_v, sem)
    products(jobs, blocks, flags, hidden_v, grad_v, total, outs, wait)


def product_scratch(jobs, hidden, width):
    return [
        pltpu.VMEM(hidden.shape, hidden.dtype),
        pltpu.VMEM((len(jobs), hidden.shape[0], width), hidden.dtype),
        pltpu.VMEM((hidden.shape[1], width), jnp.float32),
        pltpu.SemaphoreType.DMA((1 + len(jobs),)),
    ]


def product_cost(jobs, hidden, width):
    rows, ff = hidden.shape
    return pl.CostEstimate(
        flops=2 * len(jobs) * rows * ff * width,
        bytes_accessed=2 * (hidden.size + len(jobs) * (rows + ff) * width),
        transcendentals=0,
    )


def combine_kernel(recipe, blocks, n_in, flags, *refs):
    arrays, outs = refs[:n_in], refs[n_in + 1 :]
    for out, terms in zip(outs, recipe):
        total = None
        for position, flag in terms:
            value = arrays[position][...].astype(jnp.float32)
            if flag is not None:
                value = jnp.where(flags[blocks + flag] == 1, value, jnp.zeros_like(value))
            total = value if total is None else total + value
        out[...] = total.astype(out.dtype)


def place_kernel(blocks, is_hot, n_in, flags, *refs):
    arrays, out = refs[:n_in], refs[n_in + 1]
    buffer, sem = refs[n_in + 2 :]
    chunks = buffer.shape[0]
    rows = buffer.shape[1]
    hot = flags[blocks + F_HOT]
    slot = hot if is_hot else EXP_DEV - 1 - hot
    copies = []
    for c in range(chunks):
        at = slice(c * rows, (c + 1) * rows)
        total = arrays[0][at, :].astype(jnp.float32)
        for array in arrays[1:]:
            total = total + array[at, :].astype(jnp.float32)
        buffer[c] = total.astype(buffer.dtype)
        copies.append(pltpu.make_async_copy(buffer.at[c], out.at[slot, pl.ds(c * rows, rows), :], sem.at[c]))
        copies[-1].start()
    for copy in copies:
        copy.wait()


def body(hidden, grad, slots, counts, placement):
    n, holders = lax.axis_size("dp"), lax.axis_size("expert")
    (rows, ff), width, blocks = hidden.shape, grad.shape[1] // n, slots.shape[1]
    piece = jax.ShapeDtypeStruct((ff, width), jnp.bfloat16)
    quarter = holders // 4
    chain = []

    def opening(jobs):
        flags, *outs = pl.pallas_call(
            functools.partial(opening_kernel, jobs, blocks, holders),
            out_shape=[jax.ShapeDtypeStruct((blocks + F_COUNT,), jnp.int32)] + [piece] * len(jobs),
            in_specs=[HBM] * 5,
            out_specs=[SMEM] + [VMEM] * len(jobs),
            scratch_shapes=[pltpu.SMEM(a.shape, a.dtype) for a in (slots, counts, placement)]
            + product_scratch(jobs, hidden, width)
            + [pltpu.SemaphoreType.DMA((3,))],
            compiler_params=params(32),
            cost_estimate=product_cost(jobs, hidden, width),
        )(slots, counts, placement, hidden, grad)
        chain.append(outs[0])
        return flags, outs

    def product(flags, *jobs):
        outs = pl.pallas_call(
            functools.partial(product_kernel, jobs, blocks),
            out_shape=[piece] * len(jobs),
            in_specs=[SMEM, HBM, HBM, ANY],
            out_specs=[VMEM] * len(jobs),
            scratch_shapes=product_scratch(jobs, hidden, width),
            compiler_params=params(32),
            cost_estimate=product_cost(jobs, hidden, width),
        )(flags, hidden, grad, chain[-1])
        chain.append(outs[0])
        return outs

    def combine(flags, arrays, recipe):
        outs = pl.pallas_call(
            functools.partial(combine_kernel, recipe, blocks, len(arrays)),
            out_shape=[piece] * len(recipe),
            in_specs=[SMEM] + [VMEM] * len(arrays) + [ANY],
            out_specs=[VMEM] * len(recipe),
            compiler_params=params(32),
            cost_estimate=pl.CostEstimate(
                flops=len(arrays) * ff * width, bytes_accessed=2 * (len(arrays) + len(recipe)) * ff * width, transcendentals=0
            ),
        )(flags, *arrays, chain[-1])
        chain.append(outs[0])
        return outs

    def place(flags, arrays, before, is_hot):
        chunks = 4
        out = pl.pallas_call(
            functools.partial(place_kernel, blocks, is_hot, len(arrays)),
            out_shape=jax.ShapeDtypeStruct((EXP_DEV, ff, width), jnp.bfloat16),
            in_specs=[SMEM] + [VMEM] * len(arrays) + [ANY],
            out_specs=HBM,
            scratch_shapes=[pltpu.VMEM((chunks, ff // chunks, width), jnp.bfloat16), pltpu.SemaphoreType.DMA((chunks,))],
            input_output_aliases={1 + len(arrays): 0} if is_hot else {},
            compiler_params=params(32),
            cost_estimate=pl.CostEstimate(flops=3 * ff * width, bytes_accessed=8 * ff * width, transcendentals=0),
        )(flags, *arrays, before)
        chain.append(out)
        return out

    def plane(x, phase):
        pairs = []
        for k in range(holders):
            place_of, group = k // quarter, k % quarter
            pairs.append((k, (place_of ^ (1 + (group + phase) % 2)) * quarter + group))
        return lax.ppermute(x, "expert", pairs)

    def outer(x):
        return lax.ppermute(x, "dp", [(0, 1), (n - 1, n - 2)])

    def middle(x):
        return lax.ppermute(x, "dp", [(1, 2), (2, 1)])

    def both(x):
        return lax.ppermute(x, "dp", [(0, 1), (1, 0), (2, 3), (3, 2)])

    relay_of = lambda own, came: [(own, F_GOES), (came, F_PASSES)]
    add_of = lambda own, came, relayed: [(own, None), (came, F_ARRIVES), (relayed, None)]

    flags, (c3,) = opening([(COLD, 3)])
    o_c1 = outer(c3)
    (r3,) = product(flags, (REPLICA, 3))
    a1 = plane(r3, 0)
    c2, h3 = product(flags, (COLD, 2), (HOT, 3))
    o_c2 = outer(c2)
    (s3,) = combine(flags, [r3, a1], [relay_of(0, 1)])
    a2 = plane(s3, 1)
    r2, h2 = product(flags, (REPLICA, 2), (HOT, 2))
    (y,) = combine(flags, [c2, o_c1], [[(0, None), (1, None)]])
    m_c1 = middle(y)
    (h3,) = combine(flags, [h3, a1, a2], [add_of(0, 1, 2)])
    o_h1 = outer(h3)
    b1 = plane(r2, 0)
    r1, r0 = product(flags, (REPLICA, 1), (REPLICA, 0))
    (s2,) = combine(flags, [r2, b1], [relay_of(0, 1)])
    b2 = plane(s2, 1)
    c1, c0 = product(flags, (COLD, 1), (COLD, 0))
    (y,) = combine(flags, [c3, o_c2], [[(0, None), (1, None)]])
    m_c2 = middle(y)
    h1, h0 = product(flags, (HOT, 1), (HOT, 0))
    (h2,) = combine(flags, [h2, b1, b2], [add_of(0, 1, 2)])
    o_h2 = outer(h2)
    d1 = plane(jnp.stack([r1, r0]), 0)
    (x_c3,) = combine(flags, [c1, m_c1], [[(0, None), (1, None)]])
    (y,) = combine(flags, [h2, o_h1], [[(0, None), (1, None)]])
    m_h1 = middle(y)
    x_c3 = both(x_c3)
    s1, s0 = combine(flags, [r1, r0, d1[0], d1[1]], [relay_of(0, 2), relay_of(1, 3)])
    d2 = plane(jnp.stack([s1, s0]), 1)
    (y,) = combine(flags, [h3, o_h2], [[(0, None), (1, None)]])
    m_h2 = middle(y)
    x_h3, h0 = combine(
        flags, [h1, h0, d1[0], d1[1], d2[0], d2[1], m_h1], [add_of(0, 2, 4) + [(6, None)], add_of(1, 3, 5)]
    )
    x_h3 = both(x_h3)
    out = place(flags, [c0, m_c2, x_c3], chain[-1], False)
    return place(flags, [h0, m_h2, x_h3], out, True)


def solution(mesh):
    in_specs = (
        P(("dp", "expert"), None),
        P(("dp", "expert"), None),
        P(("dp", "expert"), None),
        P(("dp", "expert")),
        P(),
    )
    out_specs = P("expert", None, "dp")
    return jax.shard_map(body, mesh=mesh, in_specs=in_specs, out_specs=out_specs, check_vma=False)
```

```python
import functools

import jax
import jax.numpy as jnp
from jax import lax
from jax.experimental import pallas as pl
from jax.experimental.pallas import tpu as pltpu
from jax.sharding import PartitionSpec as P

EXP_DEV = 2
ORDER = ("c3", "r3", "c2,c10", "r2,r1,r0", "s3", "ma", "h3,h2,h10", "s2", "g3", "mb", "xc", "g2", "s1", "mx", "s0", "my", "xh", "g0", "f")
COLD, HOT, REPLICA = 0, 1, 2
SMEM = pl.BlockSpec(memory_space=pltpu.SMEM)
VMEM = pl.BlockSpec(memory_space=pltpu.VMEM)
HBM = pl.BlockSpec(memory_space=pltpu.HBM)
ANY = pl.BlockSpec(memory_space=pl.ANY)


def params(mib):
    return pltpu.CompilerParams(vmem_limit_bytes=mib << 20)


def flip_of(k, quarter, phase):
    return 1 + (k % quarter + phase) % 2


def partner(k, quarter, flip):
    return jnp.bitwise_xor(k // quarter, flip) * quarter + k % quarter


F_HOT, F_GOES, F_PASSES, F_ARRIVES, F_BLOCKS, F_COUNT = 0, 1, 2, 3, 4, 7


def write_flags(flags, slots, counts, placement, blocks, holders):
    here = lax.axis_index("expert")
    quarter = holders // 4
    group, place = lax.rem(here, quarter), lax.div(here, quarter)

    def at(flip):
        return jnp.bitwise_xor(place, flip) * quarter + group

    def home(owner):
        return lax.div(owner, EXP_DEV)

    odd = lax.rem(group, 2)
    first, second = 1 + odd, 2 - odd
    mine, sender = placement[here], placement[at(first)]
    hot = jnp.int32(EXP_DEV - 1)
    for flip in (3, 1, 2):
        owner = placement[at(flip)]
        hot = jnp.where(home(owner) == here, lax.rem(owner, EXP_DEV), hot)
    flags[blocks + F_HOT] = hot
    flags[blocks + F_GOES] = (home(mine) == at(second)).astype(jnp.int32)
    flags[blocks + F_PASSES] = (home(sender) == at(second)).astype(jnp.int32)
    flags[blocks + F_ARRIVES] = (home(sender) == here).astype(jnp.int32)
    numbers = [jnp.int32(0)] * 3
    for b in range(blocks):
        slot = slots[0, b]
        local = jnp.where((slot == EXP_DEV) & (home(mine) == here), lax.rem(mine, EXP_DEV), slot)
        kind = jnp.where(local == EXP_DEV, REPLICA, jnp.where(local == hot, HOT, COLD))
        kind = jnp.where(b < counts[0], kind, -1)
        flags[b] = kind
        rank = jnp.int32(0)
        for i in range(3):
            rank = jnp.where(kind == i, numbers[i], rank)
            numbers[i] = numbers[i] + (kind == i).astype(jnp.int32)
        flags[blocks + F_COUNT + b] = rank
    for i in range(3):
        flags[blocks + F_BLOCKS + i] = numbers[i]


def block_copies(kind, masks, blocks, flags, hidden, grad, hidden_v, grad_v, sem, start):
    rows, width = hidden_v.shape[0] // blocks, grad_v.shape[2]

    @pl.loop(0, blocks)
    def _(b):
        @pl.when(flags[b] == kind)
        def _():
            source = pl.ds(pl.multiple_of(b * rows, rows), rows)
            target = pl.ds(pl.multiple_of(flags[blocks + F_COUNT + b] * rows, rows), rows)
            copies = [pltpu.make_async_copy(hidden.at[source, :], hidden_v.at[target, :], sem.at[0, b])]
            for j, mask in enumerate(masks):
                columns = pl.ds(pl.multiple_of(jnp.bitwise_xor(lax.axis_index("dp"), mask) * width, width), width)
                copies.append(
                    pltpu.make_async_copy(grad.at[source, columns], grad_v.at[j, target, :], sem.at[1 + j, b])
                )
            for copy in copies:
                copy.start() if start else copy.wait()


def products(kind_masks, blocks, flags, hidden, grad, scratch, outs):
    outs = list(outs)
    for (kind, masks), (hidden_v, grad_v, sem) in zip(kind_masks, scratch[2:]):
        block_copies(kind, masks, blocks, flags, hidden, grad, hidden_v, grad_v, sem, True)
    turned, total = scratch[:2]
    for (kind, masks), (hidden_v, grad_v, sem) in zip(kind_masks, scratch[2:]):
        rows = hidden_v.shape[0] // blocks
        count = flags[blocks + F_BLOCKS + kind]

        @pl.when(lax.rem(count, 2) == 1)
        def _():
            at = pl.ds(pl.multiple_of(count * rows, rows), rows)
            hidden_v[at, :] = jnp.zeros((rows, hidden_v.shape[1]), hidden_v.dtype)
            for j in range(len(masks)):
                grad_v[j, at, :] = jnp.zeros((rows, grad_v.shape[2]), grad_v.dtype)

        block_copies(kind, masks, blocks, flags, hidden, grad, hidden_v, grad_v, sem, False)

        @pl.when(count == 0)
        def _():
            for j in range(len(masks)):
                total[j] = jnp.zeros(total.shape[1:], total.dtype)

        @pl.loop(0, lax.div(count + 1, 2))
        def _(i):
            at = pl.ds(pl.multiple_of(i * 2 * rows, 2 * rows), 2 * rows)
            turned[...] = jnp.transpose(hidden_v[at, :])

            @pl.loop(0, len(masks))
            def _(j):
                def product():
                    return jnp.dot(turned[...], grad_v[j, at, :], preferred_element_type=jnp.float32)

                @pl.when(i == 0)
                def _():
                    total[j] = product()

                @pl.when(i > 0)
                def _():
                    total[j] += product()

        for j in range(len(masks)):
            outs.pop(0)[...] = total[j].astype(jnp.bfloat16)


def split_outs(groups, refs):
    pieces = []
    for group, ref in zip(groups, refs):
        pieces += [ref] if len(group) == 1 else [ref.at[i] for i in range(len(group))]
    return pieces


def by_kind(groups):
    found = []
    for group in groups:
        for kind, mask in group:
            if not found or found[-1][0] != kind:
                found.append((kind, []))
            found[-1][1].append(mask)
    return found


def opening_kernel(groups, blocks, holders, slots, counts, placement, hidden, grad, flags, *refs):
    outs = split_outs(groups, refs[: len(groups)])
    slots_s, counts_s, placement_s, small, *scratch = refs[len(groups) :]
    scalars = [
        pltpu.make_async_copy(source, target, small.at[i])
        for i, (source, target) in enumerate(((slots, slots_s), (counts, counts_s), (placement, placement_s)))
    ]
    for copy in scalars:
        copy.start()
    for copy in scalars:
        copy.wait()
    write_flags(flags, slots_s, counts_s, placement_s, blocks, holders)
    products(by_kind(groups), blocks, flags, hidden, grad, pack(scratch), outs)


def product_kernel(groups, blocks, flags, hidden, grad, *refs):
    outs = split_outs(groups, refs[1 : 1 + len(groups)])
    products(by_kind(groups), blocks, flags, hidden, grad, pack(refs[1 + len(groups) :]), outs)


def pack(scratch):
    return list(scratch[:2]) + [scratch[i : i + 3] for i in range(2, len(scratch), 3)]


def product_scratch(groups, hidden, width, blocks):
    rows, ff = hidden.shape
    found = by_kind(groups)
    most = max(len(masks) for _, masks in found)
    shapes = [pltpu.VMEM((ff, 2 * rows // blocks), hidden.dtype), pltpu.VMEM((most, ff, width), jnp.float32)]
    for _, masks in found:
        shapes += [
            pltpu.VMEM(hidden.shape, hidden.dtype),
            pltpu.VMEM((len(masks), rows, width), hidden.dtype),
            pltpu.SemaphoreType.DMA((1 + len(masks), blocks)),
        ]
    return shapes


def combine_kernel(groups, blocks, n_in, flags, *refs):
    arrays = refs[:n_in]
    outs = split_outs(groups, refs[n_in + 1 :])
    recipes = [recipe for group in groups for recipe in group]
    for out, terms in zip(outs, recipes):
        total = None
        for position, index, flag in terms:
            ref = arrays[position] if index is None else arrays[position].at[index]
            value = ref[...].astype(jnp.float32)
            if flag is not None:
                value = jnp.where(flags[blocks + flag] == 1, value, jnp.zeros_like(value))
            total = value if total is None else total + value
        out[...] = total.astype(out.dtype)


def final_kernel(recipes, blocks, n_in, flags, *refs):
    arrays, out = refs[:n_in], refs[n_in]
    buffer, sem = refs[n_in + 1 :]
    _, chunks, rows, _ = buffer.shape
    hot = flags[blocks + F_HOT]
    copies = []
    for s, terms in enumerate(recipes):
        slot = hot if s == HOT else EXP_DEV - 1 - hot
        for c in range(chunks):
            at = slice(c * rows, (c + 1) * rows)
            total = None
            for position, index in terms:
                ref = arrays[position] if index is None else arrays[position].at[index]
                value = ref[at, :].astype(jnp.float32)
                total = value if total is None else total + value
            buffer[s, c] = total.astype(buffer.dtype)
            copies.append(pltpu.make_async_copy(buffer.at[s, c], out.at[slot, pl.ds(c * rows, rows), :], sem.at[s, c]))
            copies[-1].start()
    for copy in copies:
        copy.wait()


def body(*inputs):
    n, holders = lax.axis_size("dp"), lax.axis_size("expert")
    hidden, grad, slots, counts, placement = inputs
    hidden, grad, slots, placement = (
        pltpu.with_memory_space_constraint(a, pltpu.HBM) for a in (hidden, grad, slots, placement)
    )
    (rows, ff), width, blocks = hidden.shape, grad.shape[1] // n, slots.shape[1]
    quarter = holders // 4
    chain = []
    cost = pl.CostEstimate(flops=1, bytes_accessed=1, transcendentals=0)

    def shapes_of(groups):
        lead = lambda group: () if len(group) == 1 else (len(group),)
        return [jax.ShapeDtypeStruct(lead(group) + (ff, width), jnp.bfloat16) for group in groups]

    def label(groups):
        return "_".join("chr"[group[0][0]] + "".join(str(mask) for _, mask in group) for group in groups)

    def opening(*groups):
        flags, *outs = pl.pallas_call(
            functools.partial(opening_kernel, groups, blocks, holders),
            out_shape=[jax.ShapeDtypeStruct((2 * blocks + F_COUNT,), jnp.int32)] + shapes_of(groups),
            in_specs=[HBM] * 5,
            out_specs=[SMEM] + [VMEM] * len(groups),
            scratch_shapes=[pltpu.SMEM(a.shape, a.dtype) for a in (slots, counts, placement)]
            + [pltpu.SemaphoreType.DMA((3,))]
            + product_scratch(groups, hidden, width, blocks),
            compiler_params=params(32),
            cost_estimate=cost,
            name="open_" + label(groups),
        )(slots, counts, placement, hidden, grad)
        chain.append(outs[0])
        return flags, *outs

    def product(*groups):
        outs = pl.pallas_call(
            functools.partial(product_kernel, groups, blocks),
            out_shape=shapes_of(groups),
            in_specs=[SMEM, HBM, HBM, ANY],
            out_specs=[VMEM] * len(groups),
            scratch_shapes=product_scratch(groups, hidden, width, blocks),
            compiler_params=params(32),
            cost_estimate=cost,
            name="make_" + label(groups),
        )(flags, hidden, grad, chain[-1])
        chain.append(outs[0])
        return outs

    def combine(label, arrays, *groups):
        outs = pl.pallas_call(
            functools.partial(combine_kernel, groups, blocks, len(arrays)),
            out_shape=shapes_of(groups),
            in_specs=[SMEM] + [VMEM] * len(arrays) + [ANY],
            out_specs=[VMEM] * len(groups),
            compiler_params=params(32),
            cost_estimate=cost,
            name="sum_" + label,
        )(flags, *arrays, chain[-1])
        chain.append(outs[0])
        return outs

    def final(arrays, recipes):
        chunks = 4
        return pl.pallas_call(
            functools.partial(final_kernel, recipes, blocks, len(arrays)),
            out_shape=jax.ShapeDtypeStruct((EXP_DEV, ff, width), jnp.bfloat16),
            in_specs=[SMEM] + [VMEM] * len(arrays),
            out_specs=HBM,
            scratch_shapes=[
                pltpu.VMEM((EXP_DEV, chunks, ff // chunks, width), jnp.bfloat16),
                pltpu.SemaphoreType.DMA((EXP_DEV, chunks)),
            ],
            compiler_params=params(32),
            cost_estimate=cost,
            name="finish",
        )(flags, *arrays)

    def plane(x, phase):
        pairs = []
        for k in range(holders):
            place, group = k // quarter, k % quarter
            pairs.append((k, (place ^ (1 + (group + phase) % 2)) * quarter + group))
        return lax.ppermute(x, "expert", pairs)

    def outer(x):
        return lax.ppermute(x, "dp", [(0, 1), (n - 1, n - 2)])

    def middle(x):
        return lax.ppermute(x, "dp", [(1, 2), (2, 1)])

    def both(x):
        return lax.ppermute(x, "dp", [(0, 1), (1, 0), (2, 3), (3, 2)])

    value, at = {}, {}
    kinds = {"c": COLD, "h": HOT, "r": REPLICA}

    def store(name, out, pieces):
        value[name] = out
        for i, piece in enumerate(pieces):
            at[piece] = (name, i if len(pieces) > 1 else None)

    def keep(names, outs):
        for name, out in zip(names, outs):
            store(name, out, [name[0] + mask for mask in name[1:]])
            if name[0] == "r":
                store("p" + name, plane(out, 0), ["p" + mask for mask in name[1:]])
            if name[0] == "c" and name[1] in "32":
                store("o" + name, outer(out), ["oc" + mask for mask in name[1:]])

    def groups_of(names):
        return [[(kinds[name[0]], int(mask)) for mask in name[1:]] for name in names]

    def sums(label, *groups):
        names, recipes = [], []
        for group in groups:
            recipes.append([])
            for terms in group:
                recipes[-1].append([])
                for piece, flag in terms:
                    name, index = at[piece]
                    if name not in names:
                        names.append(name)
                    recipes[-1][-1].append((names.index(name), index, flag))
        return combine(label, [value[name] for name in names], *recipes)

    def gathered(mask):
        return [("h" + mask, None), ("p" + mask, F_ARRIVES), ("q" + mask, None)]

    def step(name):
        what, masks = name[0], name[1:]
        if what == "s":
            (out,) = sums(name, [[("r" + mask, F_GOES), ("p" + mask, F_PASSES)] for mask in masks])
            store("q" + name, plane(out, 1), ["q" + mask for mask in masks])
        elif what == "g":
            (out,) = sums(name, [gathered(mask) for mask in masks])
            store(name, out, ["g" + mask for mask in masks])
            if masks[0] in "32":
                store("o" + name, outer(out), ["oh" + mask for mask in masks])
        elif what == "m":
            own = {"a": "c2", "b": "c3", "x": "g2", "y": "g3"}
            come = {"a": "oc3", "b": "oc2", "x": "oh3", "y": "oh2"}
            (out,) = sums(name, [[(own[part], None), (come[part], None)] for part in masks])
            store("m" + name, middle(out), ["m" + part for part in masks])
        elif what == "x":
            whole = {"c": [("c1", None), ("ma", None)], "h": gathered("1") + [("mx", None)]}
            (out,) = sums(name, [whole[part] for part in masks])
            store("x" + name, both(out), ["x" + part for part in masks])
        elif what == "z":
            out, more = sums(name, [gathered("1") + [("mx", None)]], [gathered("0")])
            store("g0", more, ["g0"])
            store("x" + name, both(out), ["xh"])
        elif what == "f":
            (out,) = sums(name, [[("c0", None), ("mb", None), ("xc", None)]])
            store("f", out, ["f"])
        else:
            names = name.split(",")
            keep(names, product(*groups_of(names)))

    names = ORDER[0].split(",")
    flags, *outs = opening(*groups_of(names))
    keep(names, outs)
    for name in ORDER[1:]:
        step(name)
    lists = [["f"] if "f" in ORDER else ["c0", "mb", "xc"], ["g0", "my", "xh"]]
    names = sorted({at[piece][0] for pieces in lists for piece in pieces})
    recipe = [[(names.index(at[piece][0]), at[piece][1]) for piece in pieces] for pieces in lists]
    return final([value[name] for name in names], recipe)


def solution(mesh):
    in_specs = (
        P(("dp", "expert"), None),
        P(("dp", "expert"), None),
        P(("dp", "expert"), None),
        P(("dp", "expert")),
        P(),
    )
    out_specs = P("expert", None, "dp")
    return jax.shard_map(body, mesh=mesh, in_specs=in_specs, out_specs=out_specs, check_vma=False)
```

```python
import functools

import jax
import jax.numpy as jnp
from jax import lax
from jax.experimental import pallas as pl
from jax.experimental.pallas import tpu as pltpu
from jax.sharding import PartitionSpec as P

EXP_DEV = 2
ORDER = ("c3,r3", "c2,c10", "r2,r1,r0", "s3", "ma", "h3,h2,h10", "s2", "g3", "mb", "xc", "g2", "s1", "mx", "s0", "my@mb", "xh", "f", "g0")
COLD, HOT, REPLICA = 0, 1, 2
SMEM = pl.BlockSpec(memory_space=pltpu.SMEM)
VMEM = pl.BlockSpec(memory_space=pltpu.VMEM)
HBM = pl.BlockSpec(memory_space=pltpu.HBM)
ANY = pl.BlockSpec(memory_space=pl.ANY)


def params(mib):
    return pltpu.CompilerParams(vmem_limit_bytes=mib << 20)


def flip_of(k, quarter, phase):
    return 1 + (k % quarter + phase) % 2


def partner(k, quarter, flip):
    return jnp.bitwise_xor(k // quarter, flip) * quarter + k % quarter


F_HOT, F_GOES, F_PASSES, F_ARRIVES, F_BLOCKS, F_COUNT = 0, 1, 2, 3, 4, 7


def write_flags(flags, slots, counts, placement, blocks, holders):
    here = lax.axis_index("expert")
    quarter = holders // 4
    group, place = lax.rem(here, quarter), lax.div(here, quarter)

    def at(flip):
        return jnp.bitwise_xor(place, flip) * quarter + group

    def home(owner):
        return lax.div(owner, EXP_DEV)

    odd = lax.rem(group, 2)
    first, second = 1 + odd, 2 - odd
    mine, sender = placement[here], placement[at(first)]
    hot = jnp.int32(EXP_DEV - 1)
    for flip in (3, 1, 2):
        owner = placement[at(flip)]
        hot = jnp.where(home(owner) == here, lax.rem(owner, EXP_DEV), hot)
    flags[blocks + F_HOT] = hot
    flags[blocks + F_GOES] = (home(mine) == at(second)).astype(jnp.int32)
    flags[blocks + F_PASSES] = (home(sender) == at(second)).astype(jnp.int32)
    flags[blocks + F_ARRIVES] = (home(sender) == here).astype(jnp.int32)
    numbers = [jnp.int32(0)] * 3
    for b in range(blocks):
        slot = slots[0, b]
        local = jnp.where((slot == EXP_DEV) & (home(mine) == here), lax.rem(mine, EXP_DEV), slot)
        kind = jnp.where(local == EXP_DEV, REPLICA, jnp.where(local == hot, HOT, COLD))
        kind = jnp.where(b < counts[0], kind, -1)
        flags[b] = kind
        rank = jnp.int32(0)
        for i in range(3):
            rank = jnp.where(kind == i, numbers[i], rank)
            numbers[i] = numbers[i] + (kind == i).astype(jnp.int32)
        flags[blocks + F_COUNT + b] = rank
    for i in range(3):
        flags[blocks + F_BLOCKS + i] = numbers[i]


def block_copies(kind, masks, blocks, flags, hidden, grad, hidden_v, grad_v, sem, start):
    rows, width = hidden_v.shape[0] // blocks, grad_v.shape[2]

    @pl.loop(0, blocks)
    def _(b):
        @pl.when(flags[b] == kind)
        def _():
            source = pl.ds(pl.multiple_of(b * rows, rows), rows)
            target = pl.ds(pl.multiple_of(flags[blocks + F_COUNT + b] * rows, rows), rows)
            copies = [pltpu.make_async_copy(hidden.at[source, :], hidden_v.at[target, :], sem.at[0, b])]
            for j, mask in enumerate(masks):
                columns = pl.ds(pl.multiple_of(jnp.bitwise_xor(lax.axis_index("dp"), mask) * width, width), width)
                copies.append(
                    pltpu.make_async_copy(grad.at[source, columns], grad_v.at[j, target, :], sem.at[1 + j, b])
                )
            for copy in copies:
                copy.start() if start else copy.wait()


def products(kind_masks, blocks, flags, hidden, grad, scratch, outs):
    outs = list(outs)
    for (kind, masks), (hidden_v, grad_v, sem) in zip(kind_masks, scratch[2:]):
        block_copies(kind, masks, blocks, flags, hidden, grad, hidden_v, grad_v, sem, True)
    turned, total = scratch[:2]
    for (kind, masks), (hidden_v, grad_v, sem) in zip(kind_masks, scratch[2:]):
        rows = hidden_v.shape[0] // blocks
        count = flags[blocks + F_BLOCKS + kind]

        @pl.when(lax.rem(count, 2) == 1)
        def _():
            at = pl.ds(pl.multiple_of(count * rows, rows), rows)
            hidden_v[at, :] = jnp.zeros((rows, hidden_v.shape[1]), hidden_v.dtype)
            for j in range(len(masks)):
                grad_v[j, at, :] = jnp.zeros((rows, grad_v.shape[2]), grad_v.dtype)

        block_copies(kind, masks, blocks, flags, hidden, grad, hidden_v, grad_v, sem, False)

        @pl.when(count == 0)
        def _():
            for j in range(len(masks)):
                total[j] = jnp.zeros(total.shape[1:], total.dtype)

        @pl.loop(0, lax.div(count + 1, 2))
        def _(i):
            at = pl.ds(pl.multiple_of(i * 2 * rows, 2 * rows), 2 * rows)
            turned[...] = jnp.transpose(hidden_v[at, :])

            @pl.loop(0, len(masks))
            def _(j):
                def product():
                    return jnp.dot(turned[...], grad_v[j, at, :], preferred_element_type=jnp.float32)

                @pl.when(i == 0)
                def _():
                    total[j] = product()

                @pl.when(i > 0)
                def _():
                    total[j] += product()

        for j in range(len(masks)):
            outs.pop(0)[...] = total[j].astype(jnp.bfloat16)


def split_outs(groups, refs):
    pieces = []
    for group, ref in zip(groups, refs):
        pieces += [ref] if len(group) == 1 else [ref.at[i] for i in range(len(group))]
    return pieces


def by_kind(groups):
    found = []
    for group in groups:
        for kind, mask in group:
            if not found or found[-1][0] != kind:
                found.append((kind, []))
            found[-1][1].append(mask)
    return found


def opening_kernel(groups, blocks, holders, slots, counts, placement, hidden, grad, flags, *refs):
    outs = split_outs(groups, refs[: len(groups)])
    slots_s, counts_s, placement_s, small, *scratch = refs[len(groups) :]
    scalars = [
        pltpu.make_async_copy(source, target, small.at[i])
        for i, (source, target) in enumerate(((slots, slots_s), (counts, counts_s), (placement, placement_s)))
    ]
    for copy in scalars:
        copy.start()
    for copy in scalars:
        copy.wait()
    write_flags(flags, slots_s, counts_s, placement_s, blocks, holders)
    products(by_kind(groups), blocks, flags, hidden, grad, pack(scratch), outs)


def product_kernel(groups, blocks, flags, hidden, grad, *refs):
    outs = split_outs(groups, refs[1 : 1 + len(groups)])
    products(by_kind(groups), blocks, flags, hidden, grad, pack(refs[1 + len(groups) :]), outs)


def pack(scratch):
    return list(scratch[:2]) + [scratch[i : i + 3] for i in range(2, len(scratch), 3)]


def product_scratch(groups, hidden, width, blocks):
    rows, ff = hidden.shape
    found = by_kind(groups)
    most = max(len(masks) for _, masks in found)
    shapes = [pltpu.VMEM((ff, 2 * rows // blocks), hidden.dtype), pltpu.VMEM((most, ff, width), jnp.float32)]
    for _, masks in found:
        shapes += [
            pltpu.VMEM(hidden.shape, hidden.dtype),
            pltpu.VMEM((len(masks), rows, width), hidden.dtype),
            pltpu.SemaphoreType.DMA((1 + len(masks), blocks)),
        ]
    return shapes


def combine_kernel(groups, blocks, n_in, n_after, flags, *refs):
    arrays = refs[:n_in]
    outs = split_outs(groups, refs[n_in + 1 + n_after :])
    recipes = [recipe for group in groups for recipe in group]
    for out, terms in zip(outs, recipes):
        total = None
        for position, index, flag in terms:
            ref = arrays[position] if index is None else arrays[position].at[index]
            value = ref[...].astype(jnp.float32)
            if flag is not None:
                value = jnp.where(flags[blocks + flag] == 1, value, jnp.zeros_like(value))
            total = value if total is None else total + value
        out[...] = total.astype(out.dtype)


def final_kernel(recipes, blocks, n_in, flags, *refs):
    arrays, out = refs[:n_in], refs[n_in]
    buffer, sem = refs[n_in + 1 :]
    _, chunks, rows, _ = buffer.shape
    hot = flags[blocks + F_HOT]
    copies = []
    for s, terms in enumerate(recipes):
        slot = hot if s == HOT else EXP_DEV - 1 - hot
        for c in range(chunks):
            at = slice(c * rows, (c + 1) * rows)
            total = None
            for position, index in terms:
                ref = arrays[position] if index is None else arrays[position].at[index]
                value = ref[at, :].astype(jnp.float32)
                total = value if total is None else total + value
            buffer[s, c] = total.astype(buffer.dtype)
            copies.append(pltpu.make_async_copy(buffer.at[s, c], out.at[slot, pl.ds(c * rows, rows), :], sem.at[s, c]))
            copies[-1].start()
    for copy in copies:
        copy.wait()


def body(*inputs):
    n, holders = lax.axis_size("dp"), lax.axis_size("expert")
    hidden, grad, slots, counts, placement = inputs
    hidden, grad, slots, placement = (
        pltpu.with_memory_space_constraint(a, pltpu.HBM) for a in (hidden, grad, slots, placement)
    )
    (rows, ff), width, blocks = hidden.shape, grad.shape[1] // n, slots.shape[1]
    quarter = holders // 4
    chain = []
    cost = pl.CostEstimate(flops=1, bytes_accessed=1, transcendentals=0)

    def shapes_of(groups):
        lead = lambda group: () if len(group) == 1 else (len(group),)
        return [jax.ShapeDtypeStruct(lead(group) + (ff, width), jnp.bfloat16) for group in groups]

    def label(groups):
        return "_".join("chr"[group[0][0]] + "".join(str(mask) for _, mask in group) for group in groups)

    def opening(*groups):
        flags, *outs = pl.pallas_call(
            functools.partial(opening_kernel, groups, blocks, holders),
            out_shape=[jax.ShapeDtypeStruct((2 * blocks + F_COUNT,), jnp.int32)] + shapes_of(groups),
            in_specs=[HBM] * 5,
            out_specs=[SMEM] + [VMEM] * len(groups),
            scratch_shapes=[pltpu.SMEM(a.shape, a.dtype) for a in (slots, counts, placement)]
            + [pltpu.SemaphoreType.DMA((3,))]
            + product_scratch(groups, hidden, width, blocks),
            compiler_params=params(32),
            cost_estimate=cost,
            name="open_" + label(groups),
        )(slots, counts, placement, hidden, grad)
        chain.append(outs[0])
        return flags, *outs

    def product(*groups):
        outs = pl.pallas_call(
            functools.partial(product_kernel, groups, blocks),
            out_shape=shapes_of(groups),
            in_specs=[SMEM, HBM, HBM, ANY],
            out_specs=[VMEM] * len(groups),
            scratch_shapes=product_scratch(groups, hidden, width, blocks),
            compiler_params=params(32),
            cost_estimate=cost,
            name="make_" + label(groups),
        )(flags, hidden, grad, chain[-1])
        chain.append(outs[0])
        return outs

    def combine(label, arrays, *groups, after=()):
        outs = pl.pallas_call(
            functools.partial(combine_kernel, groups, blocks, len(arrays), len(after)),
            out_shape=shapes_of(groups),
            in_specs=[SMEM] + [VMEM] * len(arrays) + [ANY] * (1 + len(after)),
            out_specs=[VMEM] * len(groups),
            compiler_params=params(32),
            cost_estimate=cost,
            name="sum_" + label,
        )(flags, *arrays, chain[-1], *after)
        chain.append(outs[0])
        return outs

    def final(arrays, recipes):
        chunks = 4
        return pl.pallas_call(
            functools.partial(final_kernel, recipes, blocks, len(arrays)),
            out_shape=jax.ShapeDtypeStruct((EXP_DEV, ff, width), jnp.bfloat16),
            in_specs=[SMEM] + [VMEM] * len(arrays),
            out_specs=HBM,
            scratch_shapes=[
                pltpu.VMEM((EXP_DEV, chunks, ff // chunks, width), jnp.bfloat16),
                pltpu.SemaphoreType.DMA((EXP_DEV, chunks)),
            ],
            compiler_params=params(32),
            cost_estimate=cost,
            name="finish",
        )(flags, *arrays)

    def plane(x, phase):
        pairs = []
        for k in range(holders):
            place, group = k // quarter, k % quarter
            pairs.append((k, (place ^ (1 + (group + phase) % 2)) * quarter + group))
        return lax.ppermute(x, "expert", pairs)

    def outer(x):
        return lax.ppermute(x, "dp", [(0, 1), (n - 1, n - 2)])

    def middle(x):
        return lax.ppermute(x, "dp", [(1, 2), (2, 1)])

    def both(x):
        return lax.ppermute(x, "dp", [(0, 1), (1, 0), (2, 3), (3, 2)])

    value, at, waits = {}, {}, []
    kinds = {"c": COLD, "h": HOT, "r": REPLICA}

    def store(name, out, pieces):
        value[name] = out
        for i, piece in enumerate(pieces):
            at[piece] = (name, i if len(pieces) > 1 else None)

    def keep(names, outs):
        for name, out in zip(names, outs):
            store(name, out, [name[0] + mask for mask in name[1:]])
            if name[0] == "r":
                store("p" + name, plane(out, 0), ["p" + mask for mask in name[1:]])
            if name[0] == "c" and name[1] in "32":
                store("o" + name, outer(out), ["oc" + mask for mask in name[1:]])

    def groups_of(names):
        return [[(kinds[name[0]], int(mask)) for mask in name[1:]] for name in names]

    def sums(label, *groups):
        names, recipes = [], []
        for group in groups:
            recipes.append([])
            for terms in group:
                recipes[-1].append([])
                for piece, flag in terms:
                    name, index = at[piece]
                    if name not in names:
                        names.append(name)
                    recipes[-1][-1].append((names.index(name), index, flag))
        return combine(label, [value[name] for name in names], *recipes, after=[value[at[piece][0]] for piece in waits])

    def gathered(mask):
        return [("h" + mask, None), ("p" + mask, F_ARRIVES), ("q" + mask, None)]

    def step(name):
        nonlocal waits
        name, *waits = name.split("@")
        what, masks = name[0], name[1:]
        if what == "s":
            (out,) = sums(name, [[("r" + mask, F_GOES), ("p" + mask, F_PASSES)] for mask in masks])
            store("q" + name, plane(out, 1), ["q" + mask for mask in masks])
        elif what == "g":
            (out,) = sums(name, [gathered(mask) for mask in masks])
            store(name, out, ["g" + mask for mask in masks])
            if masks[0] in "32":
                store("o" + name, outer(out), ["oh" + mask for mask in masks])
        elif what == "m":
            own = {"a": "c2", "b": "c3", "x": "g2", "y": "g3"}
            come = {"a": "oc3", "b": "oc2", "x": "oh3", "y": "oh2"}
            (out,) = sums(name, [[(own[part], None), (come[part], None)] for part in masks])
            store("m" + name, middle(out), ["m" + part for part in masks])
        elif what == "x":
            whole = {"c": [("c1", None), ("ma", None)], "h": gathered("1") + [("mx", None)]}
            (out,) = sums(name, [whole[part] for part in masks])
            store("x" + name, both(out), ["x" + part for part in masks])
        elif what == "z":
            out, more = sums(name, [gathered("1") + [("mx", None)]], [gathered("0")])
            store("g0", more, ["g0"])
            store("x" + name, both(out), ["xh"])
        elif what == "f":
            (out,) = sums(name, [[("c0", None), ("mb", None), ("xc", None)]])
            store("f", out, ["f"])
        else:
            names = name.split(",")
            keep(names, product(*groups_of(names)))

    names = ORDER[0].split(",")
    flags, *outs = opening(*groups_of(names))
    keep(names, outs)
    for name in ORDER[1:]:
        step(name)
    lists = [["f"] if "f" in ORDER else ["c0", "mb", "xc"], ["g0", "my", "xh"]]
    names = sorted({at[piece][0] for pieces in lists for piece in pieces})
    recipe = [[(names.index(at[piece][0]), at[piece][1]) for piece in pieces] for pieces in lists]
    return final([value[name] for name in names], recipe)


def solution(mesh):
    in_specs = (
        P(("dp", "expert"), None),
        P(("dp", "expert"), None),
        P(("dp", "expert"), None),
        P(("dp", "expert")),
        P(),
    )
    out_specs = P("expert", None, "dp")
    return jax.shard_map(body, mesh=mesh, in_specs=in_specs, out_specs=out_specs, check_vma=False)
```

```python
import functools

import jax
import jax.numpy as jnp
from jax import lax
from jax.experimental import pallas as pl
from jax.experimental.pallas import tpu as pltpu
from jax.sharding import PartitionSpec as P

EXP_DEV = 2
ORDER = ("c3,r3", "c2,c10", "r2,r1,r0", "s3", "ma", "h3,h2,h10", "s2", "g3", "mb", "xc", "g2", "s1", "mx", "s0", "my@mb", "xh", "f", "g0")
COLD, HOT, REPLICA = 0, 1, 2
SMEM = pl.BlockSpec(memory_space=pltpu.SMEM)
VMEM = pl.BlockSpec(memory_space=pltpu.VMEM)
HBM = pl.BlockSpec(memory_space=pltpu.HBM)
ANY = pl.BlockSpec(memory_space=pl.ANY)


def params(mib):
    return pltpu.CompilerParams(vmem_limit_bytes=mib << 20)


def flip_of(k, quarter, phase):
    return 1 + (k % quarter + phase) % 2


def partner(k, quarter, flip):
    return jnp.bitwise_xor(k // quarter, flip) * quarter + k % quarter


F_HOT, F_GOES, F_PASSES, F_ARRIVES, F_BLOCKS, F_COUNT = 0, 1, 2, 3, 4, 7


def write_flags(flags, slots, counts, placement, blocks, holders):
    here = lax.axis_index("expert")
    quarter = holders // 4
    group, place = lax.rem(here, quarter), lax.div(here, quarter)

    def at(flip):
        return jnp.bitwise_xor(place, flip) * quarter + group

    def home(owner):
        return lax.div(owner, EXP_DEV)

    odd = lax.rem(group, 2)
    first, second = 1 + odd, 2 - odd
    mine, sender = placement[here], placement[at(first)]
    hot = jnp.int32(EXP_DEV - 1)
    for flip in (3, 1, 2):
        owner = placement[at(flip)]
        hot = jnp.where(home(owner) == here, lax.rem(owner, EXP_DEV), hot)
    flags[blocks + F_HOT] = hot
    flags[blocks + F_GOES] = (home(mine) == at(second)).astype(jnp.int32)
    flags[blocks + F_PASSES] = (home(sender) == at(second)).astype(jnp.int32)
    flags[blocks + F_ARRIVES] = (home(sender) == here).astype(jnp.int32)
    numbers = [jnp.int32(0)] * 3
    for b in range(blocks):
        slot = slots[0, b]
        local = jnp.where((slot == EXP_DEV) & (home(mine) == here), lax.rem(mine, EXP_DEV), slot)
        kind = jnp.where(local == EXP_DEV, REPLICA, jnp.where(local == hot, HOT, COLD))
        kind = jnp.where(b < counts[0], kind, -1)
        flags[b] = kind
        rank = jnp.int32(0)
        for i in range(3):
            rank = jnp.where(kind == i, numbers[i], rank)
            numbers[i] = numbers[i] + (kind == i).astype(jnp.int32)
        flags[blocks + F_COUNT + b] = rank
    for i in range(3):
        flags[blocks + F_BLOCKS + i] = numbers[i]


def block_copies(kind, masks, blocks, flags, hidden, grad, hidden_v, grad_v, sem, start):
    rows, width = hidden_v.shape[0] // blocks, grad_v.shape[2]

    @pl.loop(0, blocks)
    def _(b):
        @pl.when(flags[b] == kind)
        def _():
            source = pl.ds(pl.multiple_of(b * rows, rows), rows)
            target = pl.ds(pl.multiple_of(flags[blocks + F_COUNT + b] * rows, rows), rows)
            copies = [pltpu.make_async_copy(hidden.at[source, :], hidden_v.at[target, :], sem.at[0, b])]
            for j, mask in enumerate(masks):
                columns = pl.ds(pl.multiple_of(jnp.bitwise_xor(lax.axis_index("dp"), mask) * width, width), width)
                copies.append(
                    pltpu.make_async_copy(grad.at[source, columns], grad_v.at[j, target, :], sem.at[1 + j, b])
                )
            for copy in copies:
                copy.start() if start else copy.wait()


def products(kind_masks, blocks, flags, hidden, grad, scratch, outs):
    outs = list(outs)
    for (kind, masks), (hidden_v, grad_v, sem) in zip(kind_masks, scratch[2:]):
        block_copies(kind, masks, blocks, flags, hidden, grad, hidden_v, grad_v, sem, True)
    turned, total = scratch[:2]
    for (kind, masks), (hidden_v, grad_v, sem) in zip(kind_masks, scratch[2:]):
        rows = hidden_v.shape[0] // blocks
        count = flags[blocks + F_BLOCKS + kind]

        @pl.when(lax.rem(count, 2) == 1)
        def _():
            at = pl.ds(pl.multiple_of(count * rows, rows), rows)
            hidden_v[at, :] = jnp.zeros((rows, hidden_v.shape[1]), hidden_v.dtype)
            for j in range(len(masks)):
                grad_v[j, at, :] = jnp.zeros((rows, grad_v.shape[2]), grad_v.dtype)

        block_copies(kind, masks, blocks, flags, hidden, grad, hidden_v, grad_v, sem, False)

        @pl.when(count == 0)
        def _():
            for j in range(len(masks)):
                total[j] = jnp.zeros(total.shape[1:], total.dtype)

        @pl.loop(0, lax.div(count + 1, 2))
        def _(i):
            at = pl.ds(pl.multiple_of(i * 2 * rows, 2 * rows), 2 * rows)
            turned[...] = jnp.transpose(hidden_v[at, :])

            @pl.loop(0, len(masks))
            def _(j):
                def product():
                    return jnp.dot(turned[...], grad_v[j, at, :], preferred_element_type=jnp.float32)

                @pl.when(i == 0)
                def _():
                    total[j] = product()

                @pl.when(i > 0)
                def _():
                    total[j] += product()

        for j in range(len(masks)):
            outs.pop(0)[...] = total[j].astype(jnp.bfloat16)


def split_outs(groups, refs):
    pieces = []
    for group, ref in zip(groups, refs):
        pieces += [ref] if len(group) == 1 else [ref.at[i] for i in range(len(group))]
    return pieces


def by_kind(groups):
    found = []
    for group in groups:
        for kind, mask in group:
            if not found or found[-1][0] != kind:
                found.append((kind, []))
            found[-1][1].append(mask)
    return found


def opening_kernel(groups, blocks, holders, slots, counts, placement, hidden, grad, flags, *refs):
    outs = split_outs(groups, refs[: len(groups)])
    slots_s, counts_s, placement_s, order, turned, pair, total, hidden_v, grad_v, small, sem = refs[len(groups) :]
    found = by_kind(groups)
    rows, width = hidden_v.shape[0] // blocks, grad_v.shape[1]
    begin = pl.multiple_of(jnp.bitwise_xor(lax.axis_index("dp"), found[0][1][0]) * width, width)
    scalars = [
        pltpu.make_async_copy(source, target, small.at[i])
        for i, (source, target) in enumerate(((slots, slots_s), (counts, counts_s), (placement, placement_s)))
    ]
    loads = []
    for part in range(sem.shape[1]):
        step = hidden_v.shape[0] // sem.shape[1]
        at = pl.ds(part * step, step)
        loads.append(pltpu.make_async_copy(hidden.at[at, :], hidden_v.at[at, :], sem.at[0, part]))
        loads.append(pltpu.make_async_copy(grad.at[at, pl.ds(begin, width)], grad_v.at[at, :], sem.at[1, part]))
    for copy in scalars + loads:
        copy.start()
    for copy in scalars:
        copy.wait()
    write_flags(flags, slots_s, counts_s, placement_s, blocks, holders)
    for b in range(blocks):
        kind = flags[b]
        order[jnp.where(kind < 0, 3, kind) * blocks + flags[blocks + F_COUNT + b]] = b
    for copy in loads:
        copy.wait()
    for (kind, _), out in zip(found, outs):
        count = flags[blocks + F_BLOCKS + kind]

        @pl.when(count == 0)
        def _(out=out):
            out[...] = jnp.zeros(out.shape, out.dtype)

        @pl.loop(0, lax.div(count + 1, 2))
        def _(i, kind=kind, count=count):
            for half in range(2):
                mine = slice(half * rows, (half + 1) * rows)

                def take(half=half, mine=mine):
                    at = pl.ds(pl.multiple_of(order[kind * blocks + 2 * i + half] * rows, rows), rows)
                    turned[:, mine] = jnp.transpose(hidden_v[at, :])
                    pair[mine, :] = grad_v[at, :]

                def clear(mine=mine):
                    turned[:, mine] = jnp.zeros((turned.shape[0], rows), turned.dtype)
                    pair[mine, :] = jnp.zeros((rows, width), pair.dtype)

                if half == 0:
                    take()
                else:
                    pl.when(2 * i + 1 < count)(take)
                    pl.when(2 * i + 1 >= count)(clear)

            def product():
                return jnp.dot(turned[...], pair[...], preferred_element_type=jnp.float32)

            @pl.when(i == 0)
            def _():
                total[...] = product()

            @pl.when(i > 0)
            def _():
                total[...] += product()

        @pl.when(count > 0)
        def _(out=out):
            out[...] = total[...].astype(out.dtype)


def product_kernel(groups, blocks, flags, hidden, grad, *refs):
    outs = split_outs(groups, refs[1 : 1 + len(groups)])
    products(by_kind(groups), blocks, flags, hidden, grad, pack(refs[1 + len(groups) :]), outs)


def pack(scratch):
    return list(scratch[:2]) + [scratch[i : i + 3] for i in range(2, len(scratch), 3)]


def product_scratch(groups, hidden, width, blocks):
    rows, ff = hidden.shape
    found = by_kind(groups)
    most = max(len(masks) for _, masks in found)
    shapes = [pltpu.VMEM((ff, 2 * rows // blocks), hidden.dtype), pltpu.VMEM((most, ff, width), jnp.float32)]
    for _, masks in found:
        shapes += [
            pltpu.VMEM(hidden.shape, hidden.dtype),
            pltpu.VMEM((len(masks), rows, width), hidden.dtype),
            pltpu.SemaphoreType.DMA((1 + len(masks), blocks)),
        ]
    return shapes


def combine_kernel(groups, blocks, n_in, n_after, flags, *refs):
    arrays = refs[:n_in]
    outs = split_outs(groups, refs[n_in + 1 + n_after :])
    recipes = [recipe for group in groups for recipe in group]
    for out, terms in zip(outs, recipes):
        total = None
        for position, index, flag in terms:
            ref = arrays[position] if index is None else arrays[position].at[index]
            value = ref[...].astype(jnp.float32)
            if flag is not None:
                value = jnp.where(flags[blocks + flag] == 1, value, jnp.zeros_like(value))
            total = value if total is None else total + value
        out[...] = total.astype(out.dtype)


def place_kernel(terms, is_hot, blocks, n_in, flags, *refs):
    arrays, (out, buffer, sem) = refs[:n_in], refs[-3:]
    chunks, rows, _ = buffer.shape
    hot = flags[blocks + F_HOT]
    slot = hot if is_hot else EXP_DEV - 1 - hot
    copies = []
    for c in range(chunks):
        at = slice(c * rows, (c + 1) * rows)
        total = None
        for position, index in terms:
            ref = arrays[position] if index is None else arrays[position].at[index]
            value = ref[at, :].astype(jnp.float32)
            total = value if total is None else total + value
        buffer[c] = total.astype(buffer.dtype)
        copies.append(pltpu.make_async_copy(buffer.at[c], out.at[slot, pl.ds(c * rows, rows), :], sem.at[c]))
        copies[-1].start()
    for copy in copies:
        copy.wait()


def body(*inputs):
    n, holders = lax.axis_size("dp"), lax.axis_size("expert")
    hidden, grad, slots, counts, placement = inputs
    hidden, grad, slots, placement = (
        pltpu.with_memory_space_constraint(a, pltpu.HBM) for a in (hidden, grad, slots, placement)
    )
    (rows, ff), width, blocks = hidden.shape, grad.shape[1] // n, slots.shape[1]
    quarter = holders // 4
    chain = []
    cost = pl.CostEstimate(flops=1, bytes_accessed=1, transcendentals=0)

    def shapes_of(groups):
        lead = lambda group: () if len(group) == 1 else (len(group),)
        return [jax.ShapeDtypeStruct(lead(group) + (ff, width), jnp.bfloat16) for group in groups]

    def label(groups):
        return "_".join("chr"[group[0][0]] + "".join(str(mask) for _, mask in group) for group in groups)

    def opening(*groups):
        flags, *outs = pl.pallas_call(
            functools.partial(opening_kernel, groups, blocks, holders),
            out_shape=[jax.ShapeDtypeStruct((2 * blocks + F_COUNT,), jnp.int32)] + shapes_of(groups),
            in_specs=[HBM] * 5,
            out_specs=[SMEM] + [VMEM] * len(groups),
            scratch_shapes=[pltpu.SMEM(a.shape, a.dtype) for a in (slots, counts, placement)]
            + [
                pltpu.SMEM((4 * blocks,), jnp.int32),
                pltpu.VMEM((ff, 2 * rows // blocks), hidden.dtype),
                pltpu.VMEM((2 * rows // blocks, width), grad.dtype),
                pltpu.VMEM((ff, width), jnp.float32),
                pltpu.VMEM((rows, ff), hidden.dtype),
                pltpu.VMEM((rows, width), grad.dtype),
                pltpu.SemaphoreType.DMA((3,)),
                pltpu.SemaphoreType.DMA((2, 4)),
            ],
            compiler_params=params(32),
            cost_estimate=cost,
            name="open_" + label(groups),
        )(slots, counts, placement, hidden, grad)
        chain.append(outs[0])
        return flags, *outs

    def product(*groups):
        outs = pl.pallas_call(
            functools.partial(product_kernel, groups, blocks),
            out_shape=shapes_of(groups),
            in_specs=[SMEM, HBM, HBM, ANY],
            out_specs=[VMEM] * len(groups),
            scratch_shapes=product_scratch(groups, hidden, width, blocks),
            compiler_params=params(32),
            cost_estimate=cost,
            name="make_" + label(groups),
        )(flags, hidden, grad, chain[-1])
        chain.append(outs[0])
        return outs

    def combine(label, arrays, *groups, after=()):
        outs = pl.pallas_call(
            functools.partial(combine_kernel, groups, blocks, len(arrays), len(after)),
            out_shape=shapes_of(groups),
            in_specs=[SMEM] + [VMEM] * len(arrays) + [ANY] * (1 + len(after)),
            out_specs=[VMEM] * len(groups),
            compiler_params=params(32),
            cost_estimate=cost,
            name="sum_" + label,
        )(flags, *arrays, chain[-1], *after)
        chain.append(outs[0])
        return outs

    def place(pieces, is_hot):
        names = sorted({at[piece][0] for piece in pieces})
        terms = [(names.index(at[piece][0]), at[piece][1]) for piece in pieces]
        arrays, chunks = [value[name] for name in names], 4
        out = pl.pallas_call(
            functools.partial(place_kernel, terms, is_hot, blocks, len(arrays)),
            out_shape=jax.ShapeDtypeStruct((EXP_DEV, ff, width), jnp.bfloat16),
            in_specs=[SMEM] + [VMEM] * len(arrays) + [ANY],
            out_specs=HBM,
            scratch_shapes=[
                pltpu.VMEM((chunks, ff // chunks, width), jnp.bfloat16),
                pltpu.SemaphoreType.DMA((chunks,)),
            ],
            input_output_aliases={1 + len(arrays): 0} if is_hot else {},
            compiler_params=params(32),
            cost_estimate=cost,
            name="finish" if is_hot else "sum_f",
        )(flags, *arrays, value["out"] if is_hot else chain[-1])
        value["out"] = out
        if not is_hot:
            chain.append(out)
        return out

    def plane(x, phase):
        pairs = []
        for k in range(holders):
            place, group = k // quarter, k % quarter
            pairs.append((k, (place ^ (1 + (group + phase) % 2)) * quarter + group))
        return lax.ppermute(x, "expert", pairs)

    def outer(x):
        return lax.ppermute(x, "dp", [(0, 1), (n - 1, n - 2)])

    def middle(x):
        return lax.ppermute(x, "dp", [(1, 2), (2, 1)])

    def both(x):
        return lax.ppermute(x, "dp", [(0, 1), (1, 0), (2, 3), (3, 2)])

    value, at, waits = {}, {}, []
    kinds = {"c": COLD, "h": HOT, "r": REPLICA}

    def store(name, out, pieces):
        value[name] = out
        for i, piece in enumerate(pieces):
            at[piece] = (name, i if len(pieces) > 1 else None)

    def keep(names, outs):
        for name, out in zip(names, outs):
            store(name, out, [name[0] + mask for mask in name[1:]])
            if name[0] == "r":
                store("p" + name, plane(out, 0), ["p" + mask for mask in name[1:]])
            if name[0] == "c" and name[1] in "32":
                store("o" + name, outer(out), ["oc" + mask for mask in name[1:]])

    def groups_of(names):
        return [[(kinds[name[0]], int(mask)) for mask in name[1:]] for name in names]

    def sums(label, *groups):
        names, recipes = [], []
        for group in groups:
            recipes.append([])
            for terms in group:
                recipes[-1].append([])
                for piece, flag in terms:
                    name, index = at[piece]
                    if name not in names:
                        names.append(name)
                    recipes[-1][-1].append((names.index(name), index, flag))
        return combine(label, [value[name] for name in names], *recipes, after=[value[at[piece][0]] for piece in waits])

    def gathered(mask):
        return [("h" + mask, None), ("p" + mask, F_ARRIVES), ("q" + mask, None)]

    def step(name):
        nonlocal waits
        name, *waits = name.split("@")
        what, masks = name[0], name[1:]
        if what == "s":
            (out,) = sums(name, [[("r" + mask, F_GOES), ("p" + mask, F_PASSES)] for mask in masks])
            store("q" + name, plane(out, 1), ["q" + mask for mask in masks])
        elif what == "g":
            more = [("my", None)] if masks == "0" else []
            (out,) = sums(name, [gathered(mask) + more for mask in masks])
            store(name, out, ["g" + mask for mask in masks])
            if masks[0] in "32":
                store("o" + name, outer(out), ["oh" + mask for mask in masks])
        elif what == "m":
            own = {"a": "c2", "b": "c3", "x": "g2", "y": "g3"}
            come = {"a": "oc3", "b": "oc2", "x": "oh3", "y": "oh2"}
            (out,) = sums(name, [[(own[part], None), (come[part], None)] for part in masks])
            store("m" + name, middle(out), ["m" + part for part in masks])
        elif what == "x":
            whole = {"c": [("c1", None), ("ma", None)], "h": gathered("1") + [("mx", None)]}
            (out,) = sums(name, [whole[part] for part in masks])
            store("x" + name, both(out), ["x" + part for part in masks])
        elif what == "z":
            out, more = sums(name, [gathered("1") + [("mx", None)]], [gathered("0") + [("my", None)]])
            store("g0", more, ["g0"])
            store("x" + name, both(out), ["xh"])
        elif what == "f":
            place(["c0", "mb", "xc"], False)
        else:
            names = name.split(",")
            keep(names, product(*groups_of(names)))

    names = ORDER[0].split(",")
    flags, *outs = opening(*groups_of(names))
    keep(names, outs)
    for name in ORDER[1:]:
        step(name)
    return place(["g0", "xh"], True)


def solution(mesh):
    in_specs = (
        P(("dp", "expert"), None),
        P(("dp", "expert"), None),
        P(("dp", "expert"), None),
        P(("dp", "expert")),
        P(),
    )
    out_specs = P("expert", None, "dp")
    return jax.shard_map(body, mesh=mesh, in_specs=in_specs, out_specs=out_specs, check_vma=False)
```

```python
import functools

import jax
import jax.numpy as jnp
from jax import lax
from jax.experimental import pallas as pl
from jax.experimental.pallas import tpu as pltpu
from jax.sharding import PartitionSpec as P

EXP_DEV = 2
ORDER = ("c3,r3", "c2,c103", "r2,r1,r0", "s3", "ma", "h3,h2,h10", "s2", "g3", "mb", "xc", "g2", "s1", "mx", "s0", "my@mb", "xh", "f", "g0")
COLD, HOT, REPLICA = 0, 1, 2
SMEM = pl.BlockSpec(memory_space=pltpu.SMEM)
VMEM = pl.BlockSpec(memory_space=pltpu.VMEM)
HBM = pl.BlockSpec(memory_space=pltpu.HBM)
ANY = pl.BlockSpec(memory_space=pl.ANY)


def params(mib):
    return pltpu.CompilerParams(vmem_limit_bytes=mib << 20)


def flip_of(k, quarter, phase):
    return 1 + (k % quarter + phase) % 2


def partner(k, quarter, flip):
    return jnp.bitwise_xor(k // quarter, flip) * quarter + k % quarter


F_HOT, F_GOES, F_PASSES, F_ARRIVES, F_BLOCKS, F_COUNT = 0, 1, 2, 3, 4, 7


def write_flags(flags, slots, counts, placement, blocks, holders):
    here = lax.axis_index("expert")
    quarter = holders // 4
    group, place = lax.rem(here, quarter), lax.div(here, quarter)

    def at(flip):
        return jnp.bitwise_xor(place, flip) * quarter + group

    def home(owner):
        return lax.div(owner, EXP_DEV)

    odd = lax.rem(group, 2)
    first, second = 1 + odd, 2 - odd
    mine, sender = placement[here], placement[at(first)]
    hot = jnp.int32(EXP_DEV - 1)
    for flip in (3, 1, 2):
        owner = placement[at(flip)]
        hot = jnp.where(home(owner) == here, lax.rem(owner, EXP_DEV), hot)
    flags[blocks + F_HOT] = hot
    flags[blocks + F_GOES] = (home(mine) == at(second)).astype(jnp.int32)
    flags[blocks + F_PASSES] = (home(sender) == at(second)).astype(jnp.int32)
    flags[blocks + F_ARRIVES] = (home(sender) == here).astype(jnp.int32)
    numbers = [jnp.int32(0)] * 3
    for b in range(blocks):
        slot = slots[0, b]
        local = jnp.where((slot == EXP_DEV) & (home(mine) == here), lax.rem(mine, EXP_DEV), slot)
        kind = jnp.where(local == EXP_DEV, REPLICA, jnp.where(local == hot, HOT, COLD))
        kind = jnp.where(b < counts[0], kind, -1)
        flags[b] = kind
        rank = jnp.int32(0)
        for i in range(3):
            rank = jnp.where(kind == i, numbers[i], rank)
            numbers[i] = numbers[i] + (kind == i).astype(jnp.int32)
        flags[blocks + F_COUNT + b] = rank
    for i in range(3):
        flags[blocks + F_BLOCKS + i] = numbers[i]


def block_copies(kind, masks, blocks, flags, hidden, grad, hidden_v, grad_v, sem, start):
    rows, width = hidden_v.shape[0] // blocks, grad_v.shape[2]

    @pl.loop(0, blocks)
    def _(b):
        @pl.when(flags[b] == kind)
        def _():
            source = pl.ds(pl.multiple_of(b * rows, rows), rows)
            target = pl.ds(pl.multiple_of(flags[blocks + F_COUNT + b] * rows, rows), rows)
            copies = [pltpu.make_async_copy(hidden.at[source, :], hidden_v.at[target, :], sem.at[0, b])]
            for j, mask in enumerate(masks):
                columns = pl.ds(pl.multiple_of(jnp.bitwise_xor(lax.axis_index("dp"), mask) * width, width), width)
                copies.append(
                    pltpu.make_async_copy(grad.at[source, columns], grad_v.at[j, target, :], sem.at[1 + j, b])
                )
            for copy in copies:
                copy.start() if start else copy.wait()


def products(kind_masks, blocks, flags, hidden, grad, scratch, outs):
    outs = list(outs)
    for (kind, masks), (hidden_v, grad_v, sem) in zip(kind_masks, scratch[2:]):
        block_copies(kind, masks, blocks, flags, hidden, grad, hidden_v, grad_v, sem, True)
    turned, total = scratch[:2]
    for (kind, masks), (hidden_v, grad_v, sem) in zip(kind_masks, scratch[2:]):
        rows = hidden_v.shape[0] // blocks
        count = flags[blocks + F_BLOCKS + kind]

        @pl.when(lax.rem(count, 2) == 1)
        def _():
            at = pl.ds(pl.multiple_of(count * rows, rows), rows)
            hidden_v[at, :] = jnp.zeros((rows, hidden_v.shape[1]), hidden_v.dtype)
            for j in range(len(masks)):
                grad_v[j, at, :] = jnp.zeros((rows, grad_v.shape[2]), grad_v.dtype)

        block_copies(kind, masks, blocks, flags, hidden, grad, hidden_v, grad_v, sem, False)

        @pl.when(count == 0)
        def _():
            for j in range(len(masks)):
                total[j] = jnp.zeros(total.shape[1:], total.dtype)

        @pl.loop(0, lax.div(count + 1, 2))
        def _(i):
            at = pl.ds(pl.multiple_of(i * 2 * rows, 2 * rows), 2 * rows)
            turned[...] = jnp.transpose(hidden_v[at, :])

            @pl.loop(0, len(masks))
            def _(j):
                def product():
                    return jnp.dot(turned[...], grad_v[j, at, :], preferred_element_type=jnp.float32)

                @pl.when(i == 0)
                def _():
                    total[j] = product()

                @pl.when(i > 0)
                def _():
                    total[j] += product()

        for j in range(len(masks)):
            outs.pop(0)[...] = total[j].astype(jnp.bfloat16)


def split_outs(groups, refs):
    pieces = []
    for group, ref in zip(groups, refs):
        pieces += [ref] if len(group) == 1 else [ref.at[i] for i in range(len(group))]
    return pieces


def by_kind(groups):
    found = []
    for group in groups:
        for kind, mask in group:
            if not found or found[-1][0] != kind:
                found.append((kind, []))
            found[-1][1].append(mask)
    return found


def opening_kernel(groups, blocks, holders, slots, counts, placement, hidden, grad, flags, *refs):
    outs = split_outs(groups, refs[: len(groups)])
    slots_s, counts_s, placement_s, order, turned, pair, total, hidden_v, grad_v, small, sem = refs[len(groups) :]
    found = by_kind(groups)
    rows, width = hidden_v.shape[0] // blocks, grad_v.shape[1]
    begin = pl.multiple_of(jnp.bitwise_xor(lax.axis_index("dp"), found[0][1][0]) * width, width)
    scalars = [
        pltpu.make_async_copy(source, target, small.at[i])
        for i, (source, target) in enumerate(((slots, slots_s), (counts, counts_s), (placement, placement_s)))
    ]
    loads = []
    for part in range(sem.shape[1]):
        step = hidden_v.shape[0] // sem.shape[1]
        at = pl.ds(part * step, step)
        loads.append(pltpu.make_async_copy(hidden.at[at, :], hidden_v.at[at, :], sem.at[0, part]))
        loads.append(pltpu.make_async_copy(grad.at[at, pl.ds(begin, width)], grad_v.at[at, :], sem.at[1, part]))
    for copy in scalars + loads:
        copy.start()
    for copy in scalars:
        copy.wait()
    write_flags(flags, slots_s, counts_s, placement_s, blocks, holders)
    for b in range(blocks):
        kind = flags[b]
        order[jnp.where(kind < 0, 3, kind) * blocks + flags[blocks + F_COUNT + b]] = b
    for copy in loads:
        copy.wait()
    for (kind, _), out in zip(found, outs):
        count = flags[blocks + F_BLOCKS + kind]
        if kind == COLD:
            here, n = lax.axis_index("dp"), lax.axis_size("dp")
            count = jnp.where((here == 0) | (here == n - 1), count, 0)

        @pl.when(count == 0)
        def _(out=out):
            out[...] = jnp.zeros(out.shape, out.dtype)

        pairs = lax.div(count + 1, 2)

        @pl.loop(0, pairs)
        def _(i, kind=kind, count=count, out=out, end=pairs - 1):
            for half in range(2):
                mine = slice(half * rows, (half + 1) * rows)

                def take(half=half, mine=mine):
                    at = pl.ds(pl.multiple_of(order[kind * blocks + 2 * i + half] * rows, rows), rows)
                    turned[:, mine] = jnp.transpose(hidden_v[at, :])
                    pair[mine, :] = grad_v[at, :]

                def clear(mine=mine):
                    turned[:, mine] = jnp.zeros((turned.shape[0], rows), turned.dtype)
                    pair[mine, :] = jnp.zeros((rows, width), pair.dtype)

                if half == 0:
                    take()
                else:
                    pl.when(2 * i + 1 < count)(take)
                    pl.when(2 * i + 1 >= count)(clear)

            def product():
                return jnp.dot(turned[...], pair[...], preferred_element_type=jnp.float32)

            @pl.when((i == 0) & (i < end))
            def _():
                total[...] = product()

            @pl.when((i > 0) & (i < end))
            def _():
                total[...] += product()

            @pl.when((i == 0) & (i == end))
            def _():
                out[...] = product().astype(out.dtype)

            @pl.when((i > 0) & (i == end))
            def _():
                out[...] = (total[...] + product()).astype(out.dtype)


def product_kernel(groups, blocks, flags, hidden, grad, *refs):
    outs = split_outs(groups, refs[1 : 1 + len(groups)])
    products(by_kind(groups), blocks, flags, hidden, grad, pack(refs[1 + len(groups) :]), outs)


def pack(scratch):
    return list(scratch[:2]) + [scratch[i : i + 3] for i in range(2, len(scratch), 3)]


def product_scratch(groups, hidden, width, blocks):
    rows, ff = hidden.shape
    found = by_kind(groups)
    most = max(len(masks) for _, masks in found)
    shapes = [pltpu.VMEM((ff, 2 * rows // blocks), hidden.dtype), pltpu.VMEM((most, ff, width), jnp.float32)]
    for _, masks in found:
        shapes += [
            pltpu.VMEM(hidden.shape, hidden.dtype),
            pltpu.VMEM((len(masks), rows, width), hidden.dtype),
            pltpu.SemaphoreType.DMA((1 + len(masks), blocks)),
        ]
    return shapes


def combine_kernel(groups, blocks, n_in, n_after, flags, *refs):
    arrays = refs[:n_in]
    outs = split_outs(groups, refs[n_in + 1 + n_after :])
    recipes = [recipe for group in groups for recipe in group]
    for out, terms in zip(outs, recipes):
        total = None
        for position, index, flag in terms:
            ref = arrays[position] if index is None else arrays[position].at[index]
            value = ref[...].astype(jnp.float32)
            if flag is not None:
                value = jnp.where(flags[blocks + flag] == 1, value, jnp.zeros_like(value))
            total = value if total is None else total + value
        out[...] = total.astype(out.dtype)


def place_kernel(terms, is_hot, blocks, n_in, flags, *refs):
    arrays, (out, buffer, sem) = refs[:n_in], refs[-3:]
    chunks, rows, _ = buffer.shape
    hot = flags[blocks + F_HOT]
    slot = hot if is_hot else EXP_DEV - 1 - hot
    copies = []
    for c in range(chunks):
        at = slice(c * rows, (c + 1) * rows)
        total = None
        for position, index in terms:
            ref = arrays[position] if index is None else arrays[position].at[index]
            value = ref[at, :].astype(jnp.float32)
            total = value if total is None else total + value
        buffer[c] = total.astype(buffer.dtype)
        copies.append(pltpu.make_async_copy(buffer.at[c], out.at[slot, pl.ds(c * rows, rows), :], sem.at[c]))
        copies[-1].start()
    for copy in copies:
        copy.wait()


def body(*inputs):
    n, holders = lax.axis_size("dp"), lax.axis_size("expert")
    hidden, grad, slots, counts, placement = inputs
    hidden, grad, slots, placement = (
        pltpu.with_memory_space_constraint(a, pltpu.HBM) for a in (hidden, grad, slots, placement)
    )
    (rows, ff), width, blocks = hidden.shape, grad.shape[1] // n, slots.shape[1]
    quarter = holders // 4
    chain = []
    cost = pl.CostEstimate(flops=1, bytes_accessed=1, transcendentals=0)

    def shapes_of(groups):
        lead = lambda group: () if len(group) == 1 else (len(group),)
        return [jax.ShapeDtypeStruct(lead(group) + (ff, width), jnp.bfloat16) for group in groups]

    def label(groups):
        return "_".join("chr"[group[0][0]] + "".join(str(mask) for _, mask in group) for group in groups)

    def opening(*groups):
        flags, *outs = pl.pallas_call(
            functools.partial(opening_kernel, groups, blocks, holders),
            out_shape=[jax.ShapeDtypeStruct((2 * blocks + F_COUNT,), jnp.int32)] + shapes_of(groups),
            in_specs=[HBM] * 5,
            out_specs=[SMEM] + [VMEM] * len(groups),
            scratch_shapes=[pltpu.SMEM(a.shape, a.dtype) for a in (slots, counts, placement)]
            + [
                pltpu.SMEM((4 * blocks,), jnp.int32),
                pltpu.VMEM((ff, 2 * rows // blocks), hidden.dtype),
                pltpu.VMEM((2 * rows // blocks, width), grad.dtype),
                pltpu.VMEM((ff, width), jnp.float32),
                pltpu.VMEM((rows, ff), hidden.dtype),
                pltpu.VMEM((rows, width), grad.dtype),
                pltpu.SemaphoreType.DMA((3,)),
                pltpu.SemaphoreType.DMA((2, 4)),
            ],
            compiler_params=params(32),
            cost_estimate=cost,
            name="open_" + label(groups),
        )(slots, counts, placement, hidden, grad)
        chain.append(outs[0])
        return flags, *outs

    def product(*groups):
        outs = pl.pallas_call(
            functools.partial(product_kernel, groups, blocks),
            out_shape=shapes_of(groups),
            in_specs=[SMEM, HBM, HBM, ANY],
            out_specs=[VMEM] * len(groups),
            scratch_shapes=product_scratch(groups, hidden, width, blocks),
            compiler_params=params(32),
            cost_estimate=cost,
            name="make_" + label(groups),
        )(flags, hidden, grad, chain[-1])
        chain.append(outs[0])
        return outs

    def combine(label, arrays, *groups, after=()):
        outs = pl.pallas_call(
            functools.partial(combine_kernel, groups, blocks, len(arrays), len(after)),
            out_shape=shapes_of(groups),
            in_specs=[SMEM] + [VMEM] * len(arrays) + [ANY] * (1 + len(after)),
            out_specs=[VMEM] * len(groups),
            compiler_params=params(32),
            cost_estimate=cost,
            name="sum_" + label,
        )(flags, *arrays, chain[-1], *after)
        chain.append(outs[0])
        return outs

    def place(pieces, is_hot):
        names = sorted({at[piece][0] for piece in pieces})
        terms = [(names.index(at[piece][0]), at[piece][1]) for piece in pieces]
        arrays, chunks = [value[name] for name in names], 4
        out = pl.pallas_call(
            functools.partial(place_kernel, terms, is_hot, blocks, len(arrays)),
            out_shape=jax.ShapeDtypeStruct((EXP_DEV, ff, width), jnp.bfloat16),
            in_specs=[SMEM] + [VMEM] * len(arrays) + [ANY],
            out_specs=HBM,
            scratch_shapes=[
                pltpu.VMEM((chunks, ff // chunks, width), jnp.bfloat16),
                pltpu.SemaphoreType.DMA((chunks,)),
            ],
            input_output_aliases={1 + len(arrays): 0} if is_hot else {},
            compiler_params=params(32),
            cost_estimate=cost,
            name="finish" if is_hot else "sum_f",
        )(flags, *arrays, value["out"] if is_hot else chain[-1])
        value["out"] = out
        if not is_hot:
            chain.append(out)
        return out

    def plane(x, phase):
        pairs = []
        for k in range(holders):
            place, group = k // quarter, k % quarter
            pairs.append((k, (place ^ (1 + (group + phase) % 2)) * quarter + group))
        return lax.ppermute(x, "expert", pairs)

    def outer(x):
        return lax.ppermute(x, "dp", [(0, 1), (n - 1, n - 2)])

    def middle(x):
        return lax.ppermute(x, "dp", [(1, 2), (2, 1)])

    def both(x):
        return lax.ppermute(x, "dp", [(0, 1), (1, 0), (2, 3), (3, 2)])

    value, at, waits = {}, {}, []
    kinds = {"c": COLD, "h": HOT, "r": REPLICA}

    def store(name, out, pieces):
        value[name] = out
        for i, piece in enumerate(pieces):
            at[piece] = (name, i if len(pieces) > 1 else None)

    def keep(names, outs):
        for name, out in zip(names, outs):
            store(name, out, [name[0] + mask for mask in name[1:]])
            if name[0] == "r":
                store("p" + name, plane(out, 0), ["p" + mask for mask in name[1:]])
            if name[0] == "c" and name[1] in "32":
                store("o" + name, outer(out), ["oc" + mask for mask in name[1:]])

    def groups_of(names):
        return [[(kinds[name[0]], int(mask)) for mask in name[1:]] for name in names]

    def sums(label, *groups):
        names, recipes = [], []
        for group in groups:
            recipes.append([])
            for terms in group:
                recipes[-1].append([])
                for piece, flag in terms:
                    name, index = at[piece]
                    if name not in names:
                        names.append(name)
                    recipes[-1][-1].append((names.index(name), index, flag))
        return combine(label, [value[name] for name in names], *recipes, after=[value[at[piece][0]] for piece in waits])

    def gathered(mask):
        return [("h" + mask, None), ("p" + mask, F_ARRIVES), ("q" + mask, None)]

    def step(name):
        nonlocal waits
        name, *waits = name.split("@")
        what, masks = name[0], name[1:]
        if what == "s":
            (out,) = sums(name, [[("r" + mask, F_GOES), ("p" + mask, F_PASSES)] for mask in masks])
            store("q" + name, plane(out, 1), ["q" + mask for mask in masks])
        elif what == "g":
            more = [("my", None)] if masks == "0" else []
            (out,) = sums(name, [gathered(mask) + more for mask in masks])
            store(name, out, ["g" + mask for mask in masks])
            if masks[0] in "32":
                store("o" + name, outer(out), ["oh" + mask for mask in masks])
        elif what == "m":
            own = {"a": "c2", "b": "c3", "x": "g2", "y": "g3"}
            come = {"a": "oc3", "b": "oc2", "x": "oh3", "y": "oh2"}
            (out,) = sums(name, [[(own[part], None), (come[part], None)] for part in masks])
            store("m" + name, middle(out), ["m" + part for part in masks])
        elif what == "x":
            whole = {"c": [("c1", None), ("ma", None)], "h": gathered("1") + [("mx", None)]}
            (out,) = sums(name, [whole[part] for part in masks])
            store("x" + name, both(out), ["x" + part for part in masks])
        elif what == "z":
            out, more = sums(name, [gathered("1") + [("mx", None)]], [gathered("0") + [("my", None)]])
            store("g0", more, ["g0"])
            store("x" + name, both(out), ["xh"])
        elif what == "f":
            place(["c0", "mb", "xc"], False)
        else:
            names = name.split(",")
            keep(names, product(*groups_of(names)))

    names = ORDER[0].split(",")
    flags, *outs = opening(*groups_of(names))
    keep(names, outs)
    for name in ORDER[1:]:
        step(name)
    return place(["g0", "xh"], True)


def solution(mesh):
    in_specs = (
        P(("dp", "expert"), None),
        P(("dp", "expert"), None),
        P(("dp", "expert"), None),
        P(("dp", "expert")),
        P(),
    )
    out_specs = P("expert", None, "dp")
    return jax.shard_map(body, mesh=mesh, in_specs=in_specs, out_specs=out_specs, check_vma=False)
```

```python
import functools

import jax
import jax.numpy as jnp
from jax import lax
from jax.experimental import pallas as pl
from jax.experimental.pallas import tpu as pltpu
from jax.sharding import PartitionSpec as P

EXP_DEV = 2
ORDER = ("c3,r3", "c2,c10", "r2,r1,r0", "s3", "ma", "h3,h2,h10", "s2", "g3", "mb", "xc", "g2", "s1", "mx", "s0", "my@mb", "xh", "f", "g0")
COLD, HOT, REPLICA = 0, 1, 2
SMEM = pl.BlockSpec(memory_space=pltpu.SMEM)
VMEM = pl.BlockSpec(memory_space=pltpu.VMEM)
HBM = pl.BlockSpec(memory_space=pltpu.HBM)
ANY = pl.BlockSpec(memory_space=pl.ANY)


def params(mib):
    return pltpu.CompilerParams(vmem_limit_bytes=mib << 20)


def flip_of(k, quarter, phase):
    return 1 + (k % quarter + phase) % 2


def partner(k, quarter, flip):
    return jnp.bitwise_xor(k // quarter, flip) * quarter + k % quarter


F_HOT, F_GOES, F_PASSES, F_ARRIVES, F_BLOCKS, F_COUNT = 0, 1, 2, 3, 4, 7


def write_flags(flags, slots, counts, placement, blocks, holders):
    here = lax.axis_index("expert")
    quarter = holders // 4
    group, place = lax.rem(here, quarter), lax.div(here, quarter)

    def at(flip):
        return jnp.bitwise_xor(place, flip) * quarter + group

    def home(owner):
        return lax.div(owner, EXP_DEV)

    odd = lax.rem(group, 2)
    first, second = 1 + odd, 2 - odd
    mine, sender = placement[here], placement[at(first)]
    hot = jnp.int32(EXP_DEV - 1)
    for flip in (3, 1, 2):
        owner = placement[at(flip)]
        hot = jnp.where(home(owner) == here, lax.rem(owner, EXP_DEV), hot)
    flags[blocks + F_HOT] = hot
    flags[blocks + F_GOES] = (home(mine) == at(second)).astype(jnp.int32)
    flags[blocks + F_PASSES] = (home(sender) == at(second)).astype(jnp.int32)
    flags[blocks + F_ARRIVES] = (home(sender) == here).astype(jnp.int32)
    numbers = [jnp.int32(0)] * 3
    for b in range(blocks):
        slot = slots[0, b]
        local = jnp.where((slot == EXP_DEV) & (home(mine) == here), lax.rem(mine, EXP_DEV), slot)
        kind = jnp.where(local == EXP_DEV, REPLICA, jnp.where(local == hot, HOT, COLD))
        kind = jnp.where(b < counts[0], kind, -1)
        flags[b] = kind
        rank = jnp.int32(0)
        for i in range(3):
            rank = jnp.where(kind == i, numbers[i], rank)
            numbers[i] = numbers[i] + (kind == i).astype(jnp.int32)
        flags[blocks + F_COUNT + b] = rank
    for i in range(3):
        flags[blocks + F_BLOCKS + i] = numbers[i]


def block_copies(kind, masks, blocks, flags, hidden, grad, hidden_v, grad_v, sem, start):
    rows, width = hidden_v.shape[0] // blocks, grad_v.shape[2]

    @pl.loop(0, blocks)
    def _(b):
        @pl.when(flags[b] == kind)
        def _():
            source = pl.ds(pl.multiple_of(b * rows, rows), rows)
            target = pl.ds(pl.multiple_of(flags[blocks + F_COUNT + b] * rows, rows), rows)
            copies = [pltpu.make_async_copy(hidden.at[source, :], hidden_v.at[target, :], sem.at[0, b])]
            for j, mask in enumerate(masks):
                columns = pl.ds(pl.multiple_of(jnp.bitwise_xor(lax.axis_index("dp"), mask) * width, width), width)
                copies.append(
                    pltpu.make_async_copy(grad.at[source, columns], grad_v.at[j, target, :], sem.at[1 + j, b])
                )
            for copy in copies:
                copy.start() if start else copy.wait()


def products(kind_masks, blocks, flags, hidden, grad, scratch, outs):
    outs = list(outs)
    for (kind, masks), (hidden_v, grad_v, sem) in zip(kind_masks, scratch[2:]):
        block_copies(kind, masks, blocks, flags, hidden, grad, hidden_v, grad_v, sem, True)
    turned, total = scratch[:2]
    for (kind, masks), (hidden_v, grad_v, sem) in zip(kind_masks, scratch[2:]):
        rows = hidden_v.shape[0] // blocks
        count = flags[blocks + F_BLOCKS + kind]

        @pl.when(lax.rem(count, 2) == 1)
        def _():
            at = pl.ds(pl.multiple_of(count * rows, rows), rows)
            hidden_v[at, :] = jnp.zeros((rows, hidden_v.shape[1]), hidden_v.dtype)
            for j in range(len(masks)):
                grad_v[j, at, :] = jnp.zeros((rows, grad_v.shape[2]), grad_v.dtype)

        block_copies(kind, masks, blocks, flags, hidden, grad, hidden_v, grad_v, sem, False)

        @pl.when(count == 0)
        def _():
            for j in range(len(masks)):
                total[j] = jnp.zeros(total.shape[1:], total.dtype)

        @pl.loop(0, lax.div(count + 1, 2))
        def _(i):
            at = pl.ds(pl.multiple_of(i * 2 * rows, 2 * rows), 2 * rows)
            turned[...] = jnp.transpose(hidden_v[at, :])

            @pl.loop(0, len(masks))
            def _(j):
                def product():
                    return jnp.dot(turned[...], grad_v[j, at, :], preferred_element_type=jnp.float32)

                @pl.when(i == 0)
                def _():
                    total[j] = product()

                @pl.when(i > 0)
                def _():
                    total[j] += product()

        for j in range(len(masks)):
            outs.pop(0)[...] = total[j].astype(jnp.bfloat16)


def split_outs(groups, refs):
    pieces = []
    for group, ref in zip(groups, refs):
        pieces += [ref] if len(group) == 1 else [ref.at[i] for i in range(len(group))]
    return pieces


def by_kind(groups):
    found = []
    for group in groups:
        for kind, mask in group:
            if not found or found[-1][0] != kind:
                found.append((kind, []))
            found[-1][1].append(mask)
    return found


def opening_kernel(groups, blocks, holders, slots, counts, placement, hidden, grad, flags, *refs):
    outs = split_outs(groups, refs[: len(groups)])
    slots_s, counts_s, placement_s, order, turned, pair, total, hidden_v, grad_v, small, sem = refs[len(groups) :]
    found = by_kind(groups)
    rows, width = hidden_v.shape[0] // blocks, grad_v.shape[1]
    begin = pl.multiple_of(jnp.bitwise_xor(lax.axis_index("dp"), found[0][1][0]) * width, width)
    scalars = [
        pltpu.make_async_copy(source, target, small.at[i])
        for i, (source, target) in enumerate(((slots, slots_s), (counts, counts_s), (placement, placement_s)))
    ]
    loads = []
    for part in range(sem.shape[1]):
        step = hidden_v.shape[0] // sem.shape[1]
        at = pl.ds(part * step, step)
        loads.append(pltpu.make_async_copy(hidden.at[at, :], hidden_v.at[at, :], sem.at[0, part]))
        loads.append(pltpu.make_async_copy(grad.at[at, pl.ds(begin, width)], grad_v.at[at, :], sem.at[1, part]))
    for copy in scalars + loads:
        copy.start()
    for copy in scalars:
        copy.wait()
    write_flags(flags, slots_s, counts_s, placement_s, blocks, holders)
    for b in range(blocks):
        kind = flags[b]
        order[jnp.where(kind < 0, 3, kind) * blocks + flags[blocks + F_COUNT + b]] = b
    for copy in loads:
        copy.wait()
    for (kind, _), out in zip(found, outs):
        count = flags[blocks + F_BLOCKS + kind]

        @pl.when(count == 0)
        def _(out=out):
            out[...] = jnp.zeros(out.shape, out.dtype)

        pairs = lax.div(count + 1, 2)

        @pl.loop(0, pairs)
        def _(i, kind=kind, count=count, out=out, end=pairs - 1):
            for half in range(2):
                mine = slice(half * rows, (half + 1) * rows)

                def take(half=half, mine=mine):
                    at = pl.ds(pl.multiple_of(order[kind * blocks + 2 * i + half] * rows, rows), rows)
                    turned[:, mine] = jnp.transpose(hidden_v[at, :])
                    pair[mine, :] = grad_v[at, :]

                def clear(mine=mine):
                    turned[:, mine] = jnp.zeros((turned.shape[0], rows), turned.dtype)
                    pair[mine, :] = jnp.zeros((rows, width), pair.dtype)

                if half == 0:
                    take()
                else:
                    pl.when(2 * i + 1 < count)(take)
                    pl.when(2 * i + 1 >= count)(clear)

            def product():
                return jnp.dot(turned[...], pair[...], preferred_element_type=jnp.float32)

            @pl.when((i == 0) & (i < end))
            def _():
                total[...] = product()

            @pl.when((i > 0) & (i < end))
            def _():
                total[...] += product()

            @pl.when((i == 0) & (i == end))
            def _():
                out[...] = product().astype(out.dtype)

            @pl.when((i > 0) & (i == end))
            def _():
                out[...] = (total[...] + product()).astype(out.dtype)


def product_kernel(groups, blocks, flags, hidden, grad, *refs):
    outs = split_outs(groups, refs[1 : 1 + len(groups)])
    products(by_kind(groups), blocks, flags, hidden, grad, pack(refs[1 + len(groups) :]), outs)


def pack(scratch):
    return list(scratch[:2]) + [scratch[i : i + 3] for i in range(2, len(scratch), 3)]


def product_scratch(groups, hidden, width, blocks):
    rows, ff = hidden.shape
    found = by_kind(groups)
    most = max(len(masks) for _, masks in found)
    shapes = [pltpu.VMEM((ff, 2 * rows // blocks), hidden.dtype), pltpu.VMEM((most, ff, width), jnp.float32)]
    for _, masks in found:
        shapes += [
            pltpu.VMEM(hidden.shape, hidden.dtype),
            pltpu.VMEM((len(masks), rows, width), hidden.dtype),
            pltpu.SemaphoreType.DMA((1 + len(masks), blocks)),
        ]
    return shapes


def combine_kernel(groups, blocks, n_in, n_after, flags, *refs):
    arrays = refs[:n_in]
    outs = split_outs(groups, refs[n_in + 1 + n_after :])
    recipes = [recipe for group in groups for recipe in group]
    for out, terms in zip(outs, recipes):
        total = None
        for position, index, flag in terms:
            ref = arrays[position] if index is None else arrays[position].at[index]
            value = ref[...].astype(jnp.float32)
            if flag is not None:
                value = jnp.where(flags[blocks + flag] == 1, value, jnp.zeros_like(value))
            total = value if total is None else total + value
        out[...] = total.astype(out.dtype)


def place_kernel(terms, is_hot, blocks, n_in, flags, *refs):
    arrays, (out, buffer, sem) = refs[:n_in], refs[-3:]
    chunks, rows, _ = buffer.shape
    hot = flags[blocks + F_HOT]
    slot = hot if is_hot else EXP_DEV - 1 - hot
    copies = []
    for c in range(chunks):
        at = slice(c * rows, (c + 1) * rows)
        total = None
        for position, index in terms:
            ref = arrays[position] if index is None else arrays[position].at[index]
            value = ref[at, :].astype(jnp.float32)
            total = value if total is None else total + value
        buffer[c] = total.astype(buffer.dtype)
        copies.append(pltpu.make_async_copy(buffer.at[c], out.at[slot, pl.ds(c * rows, rows), :], sem.at[c]))
        copies[-1].start()
    for copy in copies:
        copy.wait()


def body(*inputs):
    n, holders = lax.axis_size("dp"), lax.axis_size("expert")
    hidden, grad, slots, counts, placement = inputs
    hidden, grad, slots, placement = (
        pltpu.with_memory_space_constraint(a, pltpu.HBM) for a in (hidden, grad, slots, placement)
    )
    (rows, ff), width, blocks = hidden.shape, grad.shape[1] // n, slots.shape[1]
    quarter = holders // 4
    chain = []
    cost = pl.CostEstimate(flops=1, bytes_accessed=1, transcendentals=0)

    def shapes_of(groups):
        lead = lambda group: () if len(group) == 1 else (len(group),)
        return [jax.ShapeDtypeStruct(lead(group) + (ff, width), jnp.bfloat16) for group in groups]

    def label(groups):
        return "_".join("chr"[group[0][0]] + "".join(str(mask) for _, mask in group) for group in groups)

    def opening(*groups):
        flags, *outs = pl.pallas_call(
            functools.partial(opening_kernel, groups, blocks, holders),
            out_shape=[jax.ShapeDtypeStruct((2 * blocks + F_COUNT,), jnp.int32)] + shapes_of(groups),
            in_specs=[HBM] * 5,
            out_specs=[SMEM] + [VMEM] * len(groups),
            scratch_shapes=[pltpu.SMEM(a.shape, a.dtype) for a in (slots, counts, placement)]
            + [
                pltpu.SMEM((4 * blocks,), jnp.int32),
                pltpu.VMEM((ff, 2 * rows // blocks), hidden.dtype),
                pltpu.VMEM((2 * rows // blocks, width), grad.dtype),
                pltpu.VMEM((ff, width), jnp.float32),
                pltpu.VMEM((rows, ff), hidden.dtype),
                pltpu.VMEM((rows, width), grad.dtype),
                pltpu.SemaphoreType.DMA((3,)),
                pltpu.SemaphoreType.DMA((2, 4)),
            ],
            compiler_params=params(32),
            cost_estimate=cost,
            name="open_" + label(groups),
        )(slots, counts, placement, hidden, grad)
        chain.append(outs[0])
        return flags, *outs

    def product(*groups):
        outs = pl.pallas_call(
            functools.partial(product_kernel, groups, blocks),
            out_shape=shapes_of(groups),
            in_specs=[SMEM, HBM, HBM, ANY],
            out_specs=[VMEM] * len(groups),
            scratch_shapes=product_scratch(groups, hidden, width, blocks),
            compiler_params=params(32),
            cost_estimate=cost,
            name="make_" + label(groups),
        )(flags, hidden, grad, chain[-1])
        chain.append(outs[0])
        return outs

    def combine(label, arrays, *groups, after=()):
        outs = pl.pallas_call(
            functools.partial(combine_kernel, groups, blocks, len(arrays), len(after)),
            out_shape=shapes_of(groups),
            in_specs=[SMEM] + [VMEM] * len(arrays) + [ANY] * (1 + len(after)),
            out_specs=[VMEM] * len(groups),
            compiler_params=params(32),
            cost_estimate=cost,
            name="sum_" + label,
        )(flags, *arrays, chain[-1], *after)
        chain.append(outs[0])
        return outs

    def place(pieces, is_hot):
        names = sorted({at[piece][0] for piece in pieces})
        terms = [(names.index(at[piece][0]), at[piece][1]) for piece in pieces]
        arrays, chunks = [value[name] for name in names], 4
        out = pl.pallas_call(
            functools.partial(place_kernel, terms, is_hot, blocks, len(arrays)),
            out_shape=jax.ShapeDtypeStruct((EXP_DEV, ff, width), jnp.bfloat16),
            in_specs=[SMEM] + [VMEM] * len(arrays) + [ANY],
            out_specs=HBM,
            scratch_shapes=[
                pltpu.VMEM((chunks, ff // chunks, width), jnp.bfloat16),
                pltpu.SemaphoreType.DMA((chunks,)),
            ],
            input_output_aliases={1 + len(arrays): 0} if is_hot else {},
            compiler_params=params(32),
            cost_estimate=cost,
            name="finish" if is_hot else "sum_f",
        )(flags, *arrays, value["out"] if is_hot else chain[-1])
        value["out"] = out
        if not is_hot:
            chain.append(out)
        return out

    def plane(x, phase):
        pairs = []
        for k in range(holders):
            place, group = k // quarter, k % quarter
            pairs.append((k, (place ^ (1 + (group + phase) % 2)) * quarter + group))
        return lax.ppermute(x, "expert", pairs)

    def outer(x):
        return lax.ppermute(x, "dp", [(0, 1), (n - 1, n - 2)])

    def middle(x):
        return lax.ppermute(x, "dp", [(1, 2), (2, 1)])

    def both(x):
        return lax.ppermute(x, "dp", [(0, 1), (1, 0), (2, 3), (3, 2)])

    value, at, waits = {}, {}, []
    kinds = {"c": COLD, "h": HOT, "r": REPLICA}

    def store(name, out, pieces):
        value[name] = out
        for i, piece in enumerate(pieces):
            at[piece] = (name, i if len(pieces) > 1 else None)

    def keep(names, outs):
        for name, out in zip(names, outs):
            store(name, out, [name[0] + mask for mask in name[1:]])
            if name[0] == "r":
                store("p" + name, plane(out, 0), ["p" + mask for mask in name[1:]])
            if name[0] == "c" and name[1] in "32":
                store("o" + name, outer(out), ["oc" + mask for mask in name[1:]])

    def groups_of(names):
        return [[(kinds[name[0]], int(mask)) for mask in name[1:]] for name in names]

    def sums(label, *groups):
        names, recipes = [], []
        for group in groups:
            recipes.append([])
            for terms in group:
                recipes[-1].append([])
                for piece, flag in terms:
                    name, index = at[piece]
                    if name not in names:
                        names.append(name)
                    recipes[-1][-1].append((names.index(name), index, flag))
        return combine(label, [value[name] for name in names], *recipes, after=[value[at[piece][0]] for piece in waits])

    def gathered(mask):
        return [("h" + mask, None), ("p" + mask, F_ARRIVES), ("q" + mask, None)]

    def step(name):
        nonlocal waits
        name, *waits = name.split("@")
        what, masks = name[0], name[1:]
        if what == "s":
            (out,) = sums(name, [[("r" + mask, F_GOES), ("p" + mask, F_PASSES)] for mask in masks])
            store("q" + name, plane(out, 1), ["q" + mask for mask in masks])
        elif what == "g":
            more = [("my", None)] if masks == "0" else []
            (out,) = sums(name, [gathered(mask) + more for mask in masks])
            store(name, out, ["g" + mask for mask in masks])
            if masks[0] in "32":
                store("o" + name, outer(out), ["oh" + mask for mask in masks])
        elif what == "m":
            own = {"a": "c2", "b": "c3", "x": "g2", "y": "g3"}
            come = {"a": "oc3", "b": "oc2", "x": "oh3", "y": "oh2"}
            (out,) = sums(name, [[(own[part], None), (come[part], None)] for part in masks])
            store("m" + name, middle(out), ["m" + part for part in masks])
        elif what == "x":
            whole = {"c": [("c1", None), ("ma", None)], "h": gathered("1") + [("mx", None)]}
            (out,) = sums(name, [whole[part] for part in masks])
            store("x" + name, both(out), ["x" + part for part in masks])
        elif what == "z":
            out, more = sums(name, [gathered("1") + [("mx", None)]], [gathered("0") + [("my", None)]])
            store("g0", more, ["g0"])
            store("x" + name, both(out), ["xh"])
        elif what == "f":
            place(["c0", "mb", "xc"], False)
        else:
            names = name.split(",")
            keep(names, product(*groups_of(names)))

    names = ORDER[0].split(",")
    flags, *outs = opening(*groups_of(names))
    keep(names, outs)
    for name in ORDER[1:]:
        step(name)
    return place(["g0", "xh"], True)


def solution(mesh):
    in_specs = (
        P(("dp", "expert"), None),
        P(("dp", "expert"), None),
        P(("dp", "expert"), None),
        P(("dp", "expert")),
        P(),
    )
    out_specs = P("expert", None, "dp")
    return jax.shard_map(body, mesh=mesh, in_specs=in_specs, out_specs=out_specs, check_vma=False)
```
